32 devices in a mesh: segment: 2 (over x), frames: 16 (over z, y, core).
Axes of the slice: x: 2, y: 2, z: 4, core: 2. Of those that a mesh axis runs over, the one named last changes fastest.
Arguments:
- hidden: bfloat16 [2, 4096, 1536], P('segment', 'frames'), may hold values from -3 to 3
- features: bfloat16 [1024, 768], P('frames'), may hold values from -160 to 160, as said below
- kv_weight: bfloat16 [2, 768, 3072], P('segment', None, 'frames'), may hold values from -0.21875 to 0.21875
- mod_table: float32 [2, 32, 3, 1536], P('segment'), may hold values from -4 to 4
- timestep: int32 [2, 64], P('segment', 'frames'), may hold values from 0 to 31
- block_list: int32 [2, 64, 4], P('segment', 'frames'), may hold values from 0 to 15
- block_count: int32 [2, 64], P('segment', 'frames'), may hold values from 1 to 4, as said below
Outputs:
- handed: bfloat16 [2, 4096, 1536], P('segment', 'frames')
The draws below stay inside these ranges and needn't reach their ends.
Inputs may be any that keep to these rules, and one draw needn't show every extreme that they name: `features`: drawn as normal values, rows may carry common scales; within the bounds given. `block_list`: entry j of a block's list counts when j < the block's count; the others are ignored. `block_count`: the 4 frame blocks of one device have at most 10 live list entries together, and in every section some device has exactly 10.
All inputs are finite; a program needn't handle non-finite values.
Results may differ from the reference program's by a relative error of at most 0.0044.
The reference program's roundings to bfloat16 on the way (of `queries`, `key_values`, `weights` and `output`) count: a program that leaves them out, or rounds other values in their place, can miss the bound.
Values may be sent and summed in bfloat16 or wider, within the bound.
A program may use at most 64 MiB of HBM per device.

```python
import jax
import jax.numpy as jnp
from jax import lax

HEADS = 12
HD = 128
DW = 1536
FW = 768
BLK = 64
SEL = 4
NT = 32
SEGMENTS = 2
TOKENS = 4096
QB_DEV = 4
QBLK = 64
FEATS = 1024
FBLK = 16


def draw_features(key, part):
    key_base = jax.random.fold_in(jax.random.fold_in(key, 11), 0)
    base = jax.random.normal(key_base, (FEATS, FW), jnp.float32)
    values = jnp.clip(base, -6.0, 6.0)
    return values.astype(jnp.bfloat16)


def draw_block_count(key, part):
    groups = QBLK // QB_DEV
    key_busy, key_forced, key_rank, key_light = jax.random.split(jax.random.fold_in(key, 23), 4)
    busy = jax.random.randint(key_busy, (SEGMENTS, groups), 0, 3) == 0
    forced = jax.random.randint(key_forced, (SEGMENTS, 1), 0, groups)
    busy = busy | (jnp.arange(groups, dtype=jnp.int32)[None, :] == forced)
    rank_keys = jax.random.randint(key_rank, (SEGMENTS, groups, QB_DEV), 0, 1 << 20) * QB_DEV + jnp.arange(QB_DEV, dtype=jnp.int32)
    ranks = jnp.argsort(jnp.argsort(rank_keys, axis=-1), axis=-1)
    heavy = jnp.where(ranks < QB_DEV // 2, SEL, 1)
    light = jax.random.randint(key_light, (SEGMENTS, groups, QB_DEV), 1, SEL // 2 + 1)
    counts = jnp.where(busy[:, :, None], heavy, light)
    return counts.reshape(SEGMENTS, QBLK).astype(jnp.int32)


def touch_ends(result, stream_key, least, top_value):
    longest = result.shape.index(max(result.shape))
    spots = []
    for shift in (0, 1):
        where = [jax.random.randint(jax.random.fold_in(stream_key, axis), (), 0, length) for axis, length in enumerate(result.shape)]
        where[longest] = (where[longest] + shift) % result.shape[longest]
        spots.append(tuple(where))
    return result.at[spots[0]].set(least).at[spots[1]].set(top_value)


def level_of(rng, dims, cuts, smallest, largest):
    gain, own = 1.0, jax.random.fold_in(rng, 6)
    for dim, shards_of in cuts:
        draws = jnp.exp(jax.random.uniform(jax.random.fold_in(own, dim), (shards_of,), jnp.float32, smallest / len(cuts), largest / len(cuts)))
        gain = gain * jnp.repeat(draws, dims[dim] // shards_of).reshape([-1 if axis == dim else 1 for axis in range(len(dims))])
    return gain


def centred(own_key, shape, scale, reach, cuts=(), held_as=jnp.bfloat16):
    gain = level_of(own_key, shape, cuts, -0.22, 0.18) if cuts else 1.0
    entries = jax.random.normal(own_key, shape, jnp.float32) * scale * gain
    return jnp.minimum(jnp.maximum(entries, -reach), reach).astype(held_as)


def setup_inputs(seed: int = 0) -> dict:
    key_of = jax.random.split(jax.random.key(seed), 8)
    return {
        "hidden": centred(key_of[0], (SEGMENTS, TOKENS, DW), 0.5, 3.0, ((0, 2), (1, 16))),
        "features": draw_features(jax.random.fold_in(key_of[7], 71), 0),
        "kv_weight": centred(key_of[2], (SEGMENTS, FW, 2 * DW), FW ** -0.5, 0.21875, ((0, 2), (2, 16))),
        "mod_table": centred(key_of[3], (SEGMENTS, NT, 3, DW), 1.5, 4.0, ((0, 2),), jnp.float32),
        "timestep": touch_ends(jax.random.randint(key_of[4], (SEGMENTS, QBLK), 0, NT), jax.random.fold_in(key_of[4], 1), 0, NT - 1).astype(jnp.int32),
        "block_list": touch_ends(jax.random.randint(key_of[5], (SEGMENTS, QBLK, SEL), 0, FBLK), jax.random.fold_in(key_of[5], 1), 0, FBLK - 1).astype(jnp.int32),
        "block_count": draw_block_count(jax.random.fold_in(key_of[7], 71), 0),
    }


def reference(hidden, features, kv_weight, mod_table, timestep, block_list, block_count):
    segment_outputs = []
    offsets = jnp.arange(BLK, dtype=jnp.int32)
    for segment_index in range(SEGMENTS):
        key_values = jnp.dot(features, kv_weight[segment_index], preferred_element_type=jnp.float32).astype(jnp.bfloat16)
        stream = hidden[segment_index].astype(jnp.float32)
        normed = stream * lax.rsqrt(lax.optimization_barrier(jnp.mean(stream * stream, axis=-1, keepdims=True)) + 1e-06)
        modulate = mod_table[segment_index][timestep[segment_index]]

        def attend_block(inputs):
            stream_block, normed_block, mod_block, list_blocks, list_count = inputs
            queries = (normed_block * (1.0 + mod_block[1]) + mod_block[0]).astype(jnp.bfloat16)
            query_heads = queries.reshape(BLK, HEADS, HD).astype(jnp.float32)
            row_index = (list_blocks[:, None] * BLK + offsets[None, :]).reshape(-1).astype(jnp.int32)
            gathered = key_values[row_index]
            key_heads = gathered[:, :DW].reshape(-1, HEADS, HD).astype(jnp.float32)
            value_heads = gathered[:, DW:].reshape(-1, HEADS, HD).astype(jnp.float32)
            scores = jnp.einsum('qhd,khd->hqk', query_heads, key_heads) * (1.0 / HD ** 0.5)
            key_mask = jnp.repeat(jnp.arange(SEL, dtype=jnp.int32) < list_count, BLK)
            scores = jnp.where(key_mask[None, None, :], scores, jnp.float32(-1e+30))
            top_score = lax.optimization_barrier(jnp.max(scores, axis=-1, keepdims=True))
            expo = jnp.exp(scores - top_score)
            weights = (expo / lax.optimization_barrier(jnp.sum(expo, axis=-1, keepdims=True))).astype(jnp.bfloat16)
            attended = jnp.einsum('hqk,khd->qhd', weights.astype(jnp.float32), value_heads).reshape(BLK, DW)
            return (stream_block + mod_block[2] * attended).astype(jnp.bfloat16)
        blocks_out = lax.map(attend_block, (stream.reshape(QBLK, BLK, DW), normed.reshape(QBLK, BLK, DW), modulate, block_list[segment_index], block_count[segment_index]))
        segment_outputs.append(blocks_out.reshape(TOKENS, DW))
    output = jnp.stack(segment_outputs)
    return jnp.roll(output, 1, axis=0)
```

```python
import functools

import jax
import jax.numpy as jnp
from jax import lax
from jax.experimental import pallas as pl
from jax.experimental.pallas import tpu as pltpu
from jax.sharding import PartitionSpec as P

HEADS = 12
HD = 128
BLK = 64
MESH = pl.DeviceIdType.MESH
LINE, LANES, CORES = 4, 2, 2
GROUPS = 4
GH = HEADS // GROUPS
GW = GH * HD
NT_DIMS = (((1,), (1,)), ((), ()))


def tick_kernel(
    segs,
    hidden_ref, feat_ref, w_ref, mod_ref, ts_ref, list_ref, count_ref,
    out_ref,
    fbuf, wbuf, kbuf, vbuf, qbuf, gbuf, res,
    zsem, ysem, csem, rsem, osend, orecv,
):
    me = lax.axis_index("frames")
    seg = lax.axis_index("segment")
    c = me % CORES
    y = (me // CORES) % LANES
    z = me // (CORES * LANES)
    nxt = (seg + 1) % segs
    half = wbuf.shape[1]
    nblk = hidden_ref.shape[1] // BLK

    def shard(zz, yy, cc):
        return (zz * LANES + yy) * CORES + cc

    def slot(p, s):
        return fbuf.at[s] if p == 0 else wbuf.at[2 * s + (p - 1)]

    def copy(p, s, to, sem):
        return pltpu.make_async_remote_copy(
            src_ref=slot(p, s), dst_ref=slot(p, s), send_sem=sem,
            recv_sem=rsem.at[p, s], device_id={"frames": to}, device_id_type=MESH,
        )

    def z_copy(p, s, t, up):
        return copy(p, s, shard(z + 1 if up else z - 1, y, c), zsem.at[p, t, int(up)])

    def y_copy(p, zz):
        return copy(p, shard(zz, y, c), shard(z, 1 - y, c), ysem.at[p, zz])

    def c_copy(p, zz, yy):
        return copy(p, shard(zz, yy, c), shard(z, y, 1 - c), csem.at[p, zz * LANES + yy])

    def wait_recv(p, s):
        copy(p, s, me, csem.at[0, 0]).wait_recv()

    def z_event(p, t):
        if t == 0:
            @pl.when(z > 0)
            def _():
                z_copy(p, me, 0, False).start()

            @pl.when(z < LINE - 1)
            def _():
                z_copy(p, me, 0, True).start()

            y_copy(p, z).start()
            c_copy(p, z, y).start()
            return

        @pl.when(z - t >= 0)
        def _():
            s = shard(z - t, y, c)
            wait_recv(p, s)

            @pl.when(z < LINE - 1)
            def _():
                z_copy(p, s, t, True).start()

            y_copy(p, z - t).start()
            c_copy(p, z - t, y).start()

        @pl.when(z + t <= LINE - 1)
        def _():
            s = shard(z + t, y, c)
            wait_recv(p, s)

            @pl.when(z > 0)
            def _():
                z_copy(p, s, t, False).start()

            y_copy(p, z + t).start()
            c_copy(p, z + t, y).start()

    def y_event(p, t):
        def arrive(zz):
            wait_recv(p, shard(zz, 1 - y, c))
            c_copy(p, zz, 1 - y).start()

        if t == 0:
            arrive(z)
            return

        @pl.when(z - t >= 0)
        def _():
            arrive(z - t)

        @pl.when(z + t <= LINE - 1)
        def _():
            arrive(z + t)

    def from_core(p, zz, yy):
        wait_recv(p, shard(zz, yy, 1 - c))

    def queries():
        def one(b, carry):
            rows = pl.ds(pl.multiple_of(b * BLK, BLK), BLK)
            x = hidden_ref[0, rows, :].astype(jnp.float32)
            normed = x * lax.rsqrt(jnp.mean(x * x, axis=-1, keepdims=True) + 1e-06)
            mod = mod_ref[0, ts_ref[0, b]]
            q = (normed * (1.0 + mod[1:2]) + mod[0:1]).astype(jnp.bfloat16)
            for g in range(GROUPS):
                qbuf[g, rows, :] = q[:, g * GW:(g + 1) * GW]
                gbuf[g, b] = mod[2:3, g * GW:(g + 1) * GW]
            return carry

        lax.fori_loop(0, nblk, one, 0)

    def group(zz, yy):
        g = zz * LANES + yy
        keys = wbuf[pl.ds(4 * g, 4)].reshape(4 * half, wbuf.shape[2])
        values = wbuf[pl.ds(16 + 4 * g, 4)].reshape(4 * half, wbuf.shape[2])
        step = 4
        rows_step = step * fbuf.shape[1]

        def project(r, carry):
            f = fbuf[pl.ds(r * step, step)].reshape(rows_step, fbuf.shape[2])
            for buf, weight in ((kbuf, keys), (vbuf, values)):
                part = lax.dot_general(f, weight, NT_DIMS, preferred_element_type=jnp.float32)
                buf[pl.ds(r * step, step)] = part.astype(jnp.bfloat16).reshape(step, BLK, GW)
            return carry

        lax.fori_loop(0, fbuf.shape[0] // step, project, 0)
        sel = list_ref.shape[2]
        columns = pl.ds(pl.multiple_of(g * GW, GW), GW)

        def attend(b):
            rows = pl.ds(pl.multiple_of(b * BLK, BLK), BLK)
            k = jnp.concatenate([kbuf[list_ref[0, b, j]] for j in range(sel)], axis=0)
            v = jnp.concatenate([vbuf[list_ref[0, b, j]] for j in range(sel)], axis=0)
            live = lax.broadcasted_iota(jnp.int32, (BLK, sel * BLK), 1) < count_ref[0, b] * BLK
            q = qbuf[g, rows, :]
            mixed = []
            for h in range(GH):
                part = slice(h * HD, (h + 1) * HD)
                scores = lax.dot_general(
                    q[:, part], k[:, part], NT_DIMS, preferred_element_type=jnp.float32
                )
                scores = jnp.where(live, scores * (1.0 / HD ** 0.5), jnp.float32(-1e30))
                expo = jnp.exp(scores - jnp.max(scores, axis=-1, keepdims=True))
                weights = (expo / jnp.sum(expo, axis=-1, keepdims=True)).astype(jnp.bfloat16)
                mixed.append(jnp.dot(weights, v[:, part], preferred_element_type=jnp.float32))
            x = hidden_ref[0, rows, columns].astype(jnp.float32)
            res[g, rows, :] = (x + gbuf[g, b] * jnp.concatenate(mixed, axis=1)).astype(
                jnp.bfloat16
            )

        def pair(i, carry):
            attend(2 * i)
            attend(2 * i + 1)
            return carry

        lax.fori_loop(0, nblk // 2, pair, 0)
        hand(g).start()

    def hand(g):
        columns = pl.ds(pl.multiple_of(g * GW, GW), GW)
        return pltpu.make_async_remote_copy(
            src_ref=res.at[g], dst_ref=out_ref.at[0, :, columns], send_sem=osend.at[g],
            recv_sem=orecv.at[g], device_id={"segment": nxt}, device_id_type=MESH,
        )

    fbuf[me] = feat_ref[...]
    barrier = pltpu.get_barrier_semaphore()

    def greet(**where):
        pl.semaphore_signal(barrier, inc=1, device_id=where, device_id_type=MESH)

    @pl.when(z > 0)
    def _():
        greet(frames=shard(z - 1, y, c))

    @pl.when(z < LINE - 1)
    def _():
        greet(frames=shard(z + 1, y, c))

    greet(frames=shard(z, 1 - y, c))
    greet(frames=shard(z, y, 1 - c))
    greet(segment=nxt)
    if segs > 2:
        greet(segment=(seg + segs - 1) % segs)
    ends = jnp.where(z == 0, 1, 0) + jnp.where(z == LINE - 1, 1, 0)
    pl.semaphore_wait(barrier, (5 if segs > 2 else 4) + 1 - ends)

    z_event(0, 0)
    turned = w_ref[0].T
    wbuf[2 * me] = turned[:half]
    wbuf[2 * me + 1] = turned[half:]
    z_event(1, 0)
    queries()
    z_event(0, 1)
    z_event(2, 0)
    z_event(0, 2)
    z_event(1, 1)
    y_event(0, 0)
    z_event(0, 3)
    z_event(2, 1)
    y_event(0, 1)
    y_event(0, 2)
    z_event(1, 2)
    y_event(1, 0)
    z_event(2, 2)
    y_event(0, 3)
    y_event(2, 0)
    for zz in range(LINE):
        for yy in range(LANES):
            from_core(0, zz, yy)

    def from_core_pair(zz, yy):
        for p in (1, 2):
            from_core(p, zz, yy)
            from_core(p, zz + LANES, yy)

    first, other = z % 2, 1 - z % 2
    from_core_pair(first, y)
    group(first, y)
    z_event(1, 3)
    y_event(1, 1)
    z_event(2, 3)
    y_event(2, 1)
    from_core_pair(other, y)
    group(other, y)
    y_event(1, 2)
    y_event(2, 2)
    from_core_pair(first, 1 - y)
    group(first, 1 - y)
    y_event(1, 3)
    y_event(2, 3)
    from_core_pair(other, 1 - y)
    group(other, 1 - y)

    for p in range(3):
        for t in range(LINE - 1):
            @pl.when((z - t >= 0) & (z < LINE - 1))
            def _():
                z_copy(p, me, t, True).wait_send()

            @pl.when((z + t <= LINE - 1) & (z > 0))
            def _():
                z_copy(p, me, t, False).wait_send()

        for zz in range(LINE):
            y_copy(p, zz).wait_send()
            for yy in range(LANES):
                c_copy(p, zz, yy).wait_send()
    for g in range(GROUPS):
        hand(g).wait()


def local_line(segs, hidden, features, kv_weight, mod_table, timestep, block_list, block_count):
    n = LINE * LANES * CORES
    rows, width = hidden.shape[1:]
    frows, fwidth = features.shape
    half = kv_weight.shape[2] // 2
    nblk = rows // BLK
    vmem = pl.BlockSpec(memory_space=pltpu.VMEM)
    smem = pl.BlockSpec(memory_space=pltpu.SMEM)
    bf16 = jnp.bfloat16
    return pl.pallas_call(
        functools.partial(tick_kernel, segs),
        out_shape=jax.ShapeDtypeStruct(hidden.shape, bf16),
        in_specs=[vmem, vmem, vmem, vmem, smem, smem, smem],
        out_specs=pl.BlockSpec(memory_space=pl.ANY),
        scratch_shapes=[
            pltpu.VMEM((n, frows, fwidth), bf16),
            pltpu.VMEM((2 * n, half, fwidth), bf16),
            pltpu.VMEM((n * frows // BLK, BLK, GW), bf16),
            pltpu.VMEM((n * frows // BLK, BLK, GW), bf16),
            pltpu.VMEM((GROUPS, rows, GW), bf16),
            pltpu.VMEM((GROUPS, nblk, 1, GW), jnp.float32),
            pltpu.VMEM((GROUPS, rows, GW), bf16),
            pltpu.SemaphoreType.DMA((3, LINE, 2)),
            pltpu.SemaphoreType.DMA((3, LINE)),
            pltpu.SemaphoreType.DMA((3, LINE * LANES)),
            pltpu.SemaphoreType.DMA((3, n)),
            pltpu.SemaphoreType.DMA((GROUPS,)),
            pltpu.SemaphoreType.DMA((GROUPS,)),
        ],
        compiler_params=pltpu.CompilerParams(
            collective_id=0, has_side_effects=True, vmem_limit_bytes=40 * 1024 * 1024
        ),
        cost_estimate=pl.CostEstimate(
            flops=2 * n * frows * fwidth * 2 * width, bytes_accessed=1 << 24,
            transcendentals=rows * 4 * BLK * HEADS,
        ),
    )(hidden, features, kv_weight, mod_table, timestep, block_list, block_count)


def from_behind(block, axis, distance):
    devices = range(lax.axis_size(axis))
    route = [((i - distance) % len(devices), i) for i in devices]
    return lax.ppermute(block, axis, route)


def local(hidden, features, kv_weight, mod_table, timestep, block_list, block_count):
    feature_table = lax.all_gather(features, "frames", axis=0, tiled=True)
    stream = hidden[0].astype(jnp.float32)
    tok_rows = stream.shape[0]
    feature_width = stream.shape[1]
    blocks_here = tok_rows // BLK
    normed = stream * lax.rsqrt(jnp.mean(stream * stream, axis=-1, keepdims=True) + 1e-06)
    levels = mod_table.shape[1]
    onehot = (timestep[0][:, None] == jnp.arange(levels, dtype=jnp.int32)[None, :]).astype(
        jnp.float32
    )
    modulate = jnp.sum(onehot[:, :, None, None] * mod_table[0][None], axis=1)
    normed_blocks = normed.reshape(blocks_here, BLK, feature_width)
    queries = (
        normed_blocks * (1.0 + modulate[:, 1][:, None, :]) + modulate[:, 0][:, None, :]
    ).astype(jnp.bfloat16)
    queries = queries.reshape(blocks_here, BLK, HEADS, HD)
    list_counts = block_count[0]
    list_blocks = block_list[0]
    slot_count = list_blocks.shape[1]
    offsets = jnp.arange(BLK, dtype=jnp.int32)
    inv_root = 1.0 / HD**0.5
    row_index = (list_blocks[:, :, None] * BLK + offsets[None, None, :]).reshape(-1)
    key_mask = jnp.repeat(
        jnp.arange(slot_count, dtype=jnp.int32)[None, :] < list_counts[:, None], BLK, axis=1
    )
    selected = jnp.take(feature_table, row_index, axis=0)
    key_values = jnp.dot(
        selected,
        lax.all_gather(kv_weight[0], "frames", axis=1, tiled=True),
        preferred_element_type=jnp.float32,
    ).astype(jnp.bfloat16)
    key_heads = key_values[:, :feature_width].reshape(-1, HEADS, HD)
    value_heads = key_values[:, feature_width:].reshape(-1, HEADS, HD)
    keys_part = key_heads.reshape(blocks_here, -1, HEADS, HD)
    values_part = value_heads.reshape(blocks_here, -1, HEADS, HD)
    scores = jnp.einsum("bqhd,bkhd->bhqk", queries, keys_part, preferred_element_type=jnp.float32)
    softmax_scores = scores
    softmax_scores = jnp.where(
        key_mask[:, None, None, :], softmax_scores * inv_root, jnp.float32(-1e30)
    )
    top_score = jnp.max(softmax_scores, axis=-1, keepdims=True)
    expo = jnp.exp(softmax_scores - top_score)
    weights = (expo / jnp.sum(expo, axis=-1, keepdims=True)).astype(jnp.bfloat16)
    mixed_heads = jnp.einsum(
        "bhqk,bkhd->bqhd", weights, values_part, preferred_element_type=jnp.float32
    )
    part_blocks = blocks_here - 0
    mixed_rows = mixed_heads.reshape(part_blocks * BLK, feature_width)
    gate_rows = jnp.repeat(modulate[0:blocks_here, 2], BLK, axis=0)
    result = (stream + gate_rows * mixed_rows).astype(jnp.bfloat16)
    handed = from_behind(result[None], "segment", 1)
    return handed


def solution(mesh):
    placed = (
        P("segment", "frames", None),
        P("frames", None),
        P("segment", None, "frames"),
        P("segment", None, None, None),
        P("segment", "frames"),
        P("segment", "frames", None),
        P("segment", "frames"),
    )
    step = local
    if mesh.shape["frames"] == LINE * LANES * CORES:
        step = functools.partial(local_line, mesh.shape["segment"])
    return jax.shard_map(
        step, mesh=mesh, in_specs=placed, out_specs=P("segment", "frames", None), check_vma=False
    )
```

```python
import functools

import jax
import jax.numpy as jnp
from jax import lax
from jax.experimental import pallas as pl
from jax.experimental.pallas import tpu as pltpu
from jax.sharding import PartitionSpec as P

HEADS = 12
HD = 128
BLK = 64
MESH = pl.DeviceIdType.MESH
LINE, LANES, CORES = 4, 2, 2
GROUPS = 4
GH = HEADS // GROUPS
GW = GH * HD
NT_DIMS = (((1,), (1,)), ((), ()))


def tick_kernel(
    segs,
    hidden_ref, feat_ref, w_ref, mod_ref, ts_ref, list_ref, count_ref,
    out_ref,
    hbuf, mbuf, fbuf, wbuf, kv, qbuf, gbuf, res,
    zsem, ysem, csem, rsem, osend, orecv, lsem,
):
    me = lax.axis_index("frames")
    seg = lax.axis_index("segment")
    c = me % CORES
    y = (me // CORES) % LANES
    z = me // (CORES * LANES)
    nxt = (seg + 1) % segs
    half = wbuf.shape[1]
    nblk = hidden_ref.shape[1] // BLK

    def shard(zz, yy, cc):
        return (zz * LANES + yy) * CORES + cc

    def slot(p, s):
        return fbuf.at[s] if p == 0 else wbuf.at[2 * s + (p - 1)]

    def copy(p, s, to, sem):
        return pltpu.make_async_remote_copy(
            src_ref=slot(p, s), dst_ref=slot(p, s), send_sem=sem,
            recv_sem=rsem.at[p, s], device_id={"frames": to}, device_id_type=MESH,
        )

    def z_copy(p, s, t, up):
        return copy(p, s, shard(z + 1 if up else z - 1, y, c), zsem.at[p, t, int(up)])

    def y_copy(p, zz):
        return copy(p, shard(zz, y, c), shard(z, 1 - y, c), ysem.at[p, zz])

    def c_copy(p, zz, yy):
        return copy(p, shard(zz, yy, c), shard(z, y, 1 - c), csem.at[p, zz * LANES + yy])

    def wait_recv(p, s):
        copy(p, s, me, csem.at[0, 0]).wait_recv()

    def z_event(p, t):
        if t == 0:
            @pl.when(z > 0)
            def _():
                z_copy(p, me, 0, False).start()

            @pl.when(z < LINE - 1)
            def _():
                z_copy(p, me, 0, True).start()

            y_copy(p, z).start()
            c_copy(p, z, y).start()
            return

        @pl.when(z - t >= 0)
        def _():
            s = shard(z - t, y, c)
            wait_recv(p, s)

            @pl.when(z < LINE - 1)
            def _():
                z_copy(p, s, t, True).start()

            y_copy(p, z - t).start()
            c_copy(p, z - t, y).start()

        @pl.when(z + t <= LINE - 1)
        def _():
            s = shard(z + t, y, c)
            wait_recv(p, s)

            @pl.when(z > 0)
            def _():
                z_copy(p, s, t, False).start()

            y_copy(p, z + t).start()
            c_copy(p, z + t, y).start()

    def y_event(p, t):
        def arrive(zz):
            wait_recv(p, shard(zz, 1 - y, c))
            c_copy(p, zz, 1 - y).start()

        if t == 0:
            arrive(z)
            return

        @pl.when(z - t >= 0)
        def _():
            arrive(z - t)

        @pl.when(z + t <= LINE - 1)
        def _():
            arrive(z + t)

    def from_core(p, zz, yy):
        wait_recv(p, shard(zz, yy, 1 - c))

    def queries():
        def one(b, carry):
            rows = pl.ds(pl.multiple_of(b * BLK, BLK), BLK)
            x = hbuf[rows, :].astype(jnp.float32)
            normed = x * lax.rsqrt(jnp.mean(x * x, axis=-1, keepdims=True) + 1e-06)
            level = ts_ref[0, b]
            shift, scale, gate = (mbuf[i, level].reshape(1, -1) for i in range(3))
            q = (normed * (1.0 + scale) + shift).astype(jnp.bfloat16)
            for g in range(GROUPS):
                qbuf[g, rows, :] = q[:, g * GW:(g + 1) * GW]
                gbuf[g, b] = gate[:, g * GW:(g + 1) * GW]
            return carry

        lax.fori_loop(0, nblk, one, 0)

    def project(zz, yy):
        pair = zz * LANES + yy
        weight = wbuf[pl.ds(4 * pair, 4)].reshape(4 * half, wbuf.shape[2])
        step = 4
        rows_step = step * fbuf.shape[1]

        def one(r, carry):
            f = fbuf[pl.ds(r * step, step)].reshape(rows_step, fbuf.shape[2])
            part = lax.dot_general(f, weight, NT_DIMS, preferred_element_type=jnp.float32)
            kv[pair, pl.ds(r * step, step)] = part.astype(jnp.bfloat16).reshape(step, BLK, GW)
            return carry

        lax.fori_loop(0, fbuf.shape[0] // step, one, 0)

    def group(zz, yy):
        g = zz * LANES + yy
        sel = list_ref.shape[2]
        columns = pl.ds(pl.multiple_of(g * GW, GW), GW)

        for b in range(nblk):
            rows = slice(b * BLK, (b + 1) * BLK)
            k = jnp.concatenate([kv[g, list_ref[0, b, j]] for j in range(sel)], axis=0)
            v = jnp.concatenate([kv[GROUPS + g, list_ref[0, b, j]] for j in range(sel)], axis=0)
            live = lax.broadcasted_iota(jnp.int32, (BLK, sel * BLK), 1) < count_ref[0, b] * BLK
            q = qbuf[g, rows, :]
            mixed = []
            for h in range(GH):
                part = slice(h * HD, (h + 1) * HD)
                scores = lax.dot_general(
                    q[:, part], k[:, part], NT_DIMS, preferred_element_type=jnp.float32
                )
                scores = jnp.where(live, scores * (1.0 / HD ** 0.5), jnp.float32(-1e30))
                expo = jnp.exp(scores - jnp.max(scores, axis=-1, keepdims=True))
                weights = (expo * (1.0 / jnp.sum(expo, axis=-1, keepdims=True))).astype(jnp.bfloat16)
                mixed.append(jnp.dot(weights, v[:, part], preferred_element_type=jnp.float32))
            x = hbuf[rows, columns].astype(jnp.float32)
            res[g, rows, :] = (x + gbuf[g, b] * jnp.concatenate(mixed, axis=1)).astype(
                jnp.bfloat16
            )
        hand(g).start()

    def hand(g):
        columns = pl.ds(pl.multiple_of(g * GW, GW), GW)
        return pltpu.make_async_remote_copy(
            src_ref=res.at[g], dst_ref=out_ref.at[0, :, columns], send_sem=osend.at[g],
            recv_sem=orecv.at[g], device_id={"segment": nxt}, device_id_type=MESH,
        )

    loads = [
        pltpu.make_async_copy(src, dst, lsem.at[i])
        for i, (src, dst) in enumerate((
            (feat_ref, fbuf.at[me]),
            (w_ref.at[0, pl.ds(0, half)], wbuf.at[2 * me]),
            (w_ref.at[0, pl.ds(half, half)], wbuf.at[2 * me + 1]),
            (hidden_ref.at[0], hbuf),
            (mod_ref.at[0], mbuf),
        ))
    ]
    for load in loads:
        load.start()
    barrier = pltpu.get_barrier_semaphore()

    def greet(**where):
        pl.semaphore_signal(barrier, inc=1, device_id=where, device_id_type=MESH)

    @pl.when(z > 0)
    def _():
        greet(frames=shard(z - 1, y, c))

    @pl.when(z < LINE - 1)
    def _():
        greet(frames=shard(z + 1, y, c))

    greet(frames=shard(z, 1 - y, c))
    greet(frames=shard(z, y, 1 - c))
    greet(segment=nxt)
    if segs > 2:
        greet(segment=(seg + segs - 1) % segs)
    ends = jnp.where(z == 0, 1, 0) + jnp.where(z == LINE - 1, 1, 0)
    pl.semaphore_wait(barrier, (5 if segs > 2 else 4) + 1 - ends)

    loads[0].wait()
    z_event(0, 0)
    loads[1].wait()
    z_event(1, 0)
    loads[2].wait()
    loads[3].wait()
    loads[4].wait()
    queries()
    z_event(0, 1)
    z_event(2, 0)
    z_event(0, 2)
    z_event(1, 1)
    y_event(0, 0)
    z_event(0, 3)
    z_event(2, 1)
    y_event(0, 1)
    y_event(0, 2)
    z_event(1, 2)
    y_event(0, 3)
    for zz in range(LINE):
        for yy in range(LANES):
            from_core(0, zz, yy)

    def columns_in(zz, yy):
        for p in (1, 2):
            from_core(p, zz, yy)
        project(zz, yy)

    order = (
        z,
        jnp.where(z == 0, 1, z - 1),
        jnp.where(z == 3, 1, jnp.where(z == 2, 3, 2)),
        jnp.where(z < 2, 3, 0),
    )
    first, other = z // 2, 1 - z // 2
    columns_in(order[0], y)
    z_event(2, 2)
    columns_in(order[1], y)
    y_event(1, 0)
    z_event(1, 3)
    y_event(2, 0)
    columns_in(order[2], y)
    z_event(2, 3)
    group(first, y)
    y_event(1, 1)
    y_event(2, 1)
    columns_in(order[0], 1 - y)
    columns_in(order[3], y)
    group(other, y)
    columns_in(order[1], 1 - y)
    y_event(1, 2)
    y_event(2, 2)
    columns_in(order[2], 1 - y)
    group(first, 1 - y)
    y_event(1, 3)
    y_event(2, 3)
    columns_in(order[3], 1 - y)
    group(other, 1 - y)

    for p in range(3):
        for t in range(LINE - 1):
            @pl.when((z - t >= 0) & (z < LINE - 1))
            def _():
                z_copy(p, me, t, True).wait_send()

            @pl.when((z + t <= LINE - 1) & (z > 0))
            def _():
                z_copy(p, me, t, False).wait_send()

        for zz in range(LINE):
            y_copy(p, zz).wait_send()
            for yy in range(LANES):
                c_copy(p, zz, yy).wait_send()
    for g in range(GROUPS):
        hand(g).wait()


def local_line(segs, hidden, features, kv_weight, mod_table, timestep, block_list, block_count):
    n = LINE * LANES * CORES
    rows, width = hidden.shape[1:]
    frows, fwidth = features.shape
    half = kv_weight.shape[2] // 2
    kv_weight = jnp.swapaxes(kv_weight, 1, 2)
    mod_table = jnp.swapaxes(mod_table, 1, 2)
    nblk = rows // BLK
    hbm = pl.BlockSpec(memory_space=pl.ANY)
    smem = pl.BlockSpec(memory_space=pltpu.SMEM)
    bf16 = jnp.bfloat16
    return pl.pallas_call(
        functools.partial(tick_kernel, segs),
        out_shape=jax.ShapeDtypeStruct(hidden.shape, bf16),
        in_specs=[hbm, hbm, hbm, hbm, smem, smem, smem],
        out_specs=hbm,
        scratch_shapes=[
            pltpu.VMEM((rows, width), bf16),
            pltpu.VMEM(mod_table.shape[1:], jnp.float32),
            pltpu.VMEM((n, frows, fwidth), bf16),
            pltpu.VMEM((2 * n, half, fwidth), bf16),
            pltpu.VMEM((2 * GROUPS, n * frows // BLK, BLK, GW), bf16),
            pltpu.VMEM((GROUPS, rows, GW), bf16),
            pltpu.VMEM((GROUPS, nblk, 1, GW), jnp.float32),
            pltpu.VMEM((GROUPS, rows, GW), bf16),
            pltpu.SemaphoreType.DMA((3, LINE, 2)),
            pltpu.SemaphoreType.DMA((3, LINE)),
            pltpu.SemaphoreType.DMA((3, LINE * LANES)),
            pltpu.SemaphoreType.DMA((3, n)),
            pltpu.SemaphoreType.DMA((GROUPS,)),
            pltpu.SemaphoreType.DMA((GROUPS,)),
            pltpu.SemaphoreType.DMA((5,)),
        ],
        compiler_params=pltpu.CompilerParams(
            collective_id=0, has_side_effects=True, vmem_limit_bytes=60 * 1024 * 1024
        ),
        cost_estimate=pl.CostEstimate(
            flops=2 * n * frows * fwidth * 2 * width, bytes_accessed=1 << 24,
            transcendentals=rows * 4 * BLK * HEADS,
        ),
    )(hidden, features, kv_weight, mod_table, timestep, block_list, block_count)


def from_behind(block, axis, distance):
    devices = range(lax.axis_size(axis))
    route = [((i - distance) % len(devices), i) for i in devices]
    return lax.ppermute(block, axis, route)


def local(hidden, features, kv_weight, mod_table, timestep, block_list, block_count):
    feature_table = lax.all_gather(features, "frames", axis=0, tiled=True)
    stream = hidden[0].astype(jnp.float32)
    tok_rows = stream.shape[0]
    feature_width = stream.shape[1]
    blocks_here = tok_rows // BLK
    normed = stream * lax.rsqrt(jnp.mean(stream * stream, axis=-1, keepdims=True) + 1e-06)
    levels = mod_table.shape[1]
    onehot = (timestep[0][:, None] == jnp.arange(levels, dtype=jnp.int32)[None, :]).astype(
        jnp.float32
    )
    modulate = jnp.sum(onehot[:, :, None, None] * mod_table[0][None], axis=1)
    normed_blocks = normed.reshape(blocks_here, BLK, feature_width)
    queries = (
        normed_blocks * (1.0 + modulate[:, 1][:, None, :]) + modulate[:, 0][:, None, :]
    ).astype(jnp.bfloat16)
    queries = queries.reshape(blocks_here, BLK, HEADS, HD)
    list_counts = block_count[0]
    list_blocks = block_list[0]
    slot_count = list_blocks.shape[1]
    offsets = jnp.arange(BLK, dtype=jnp.int32)
    inv_root = 1.0 / HD**0.5
    row_index = (list_blocks[:, :, None] * BLK + offsets[None, None, :]).reshape(-1)
    key_mask = jnp.repeat(
        jnp.arange(slot_count, dtype=jnp.int32)[None, :] < list_counts[:, None], BLK, axis=1
    )
    selected = jnp.take(feature_table, row_index, axis=0)
    key_values = jnp.dot(
        selected,
        lax.all_gather(kv_weight[0], "frames", axis=1, tiled=True),
        preferred_element_type=jnp.float32,
    ).astype(jnp.bfloat16)
    key_heads = key_values[:, :feature_width].reshape(-1, HEADS, HD)
    value_heads = key_values[:, feature_width:].reshape(-1, HEADS, HD)
    keys_part = key_heads.reshape(blocks_here, -1, HEADS, HD)
    values_part = value_heads.reshape(blocks_here, -1, HEADS, HD)
    scores = jnp.einsum("bqhd,bkhd->bhqk", queries, keys_part, preferred_element_type=jnp.float32)
    softmax_scores = scores
    softmax_scores = jnp.where(
        key_mask[:, None, None, :], softmax_scores * inv_root, jnp.float32(-1e30)
    )
    top_score = jnp.max(softmax_scores, axis=-1, keepdims=True)
    expo = jnp.exp(softmax_scores - top_score)
    weights = (expo / jnp.sum(expo, axis=-1, keepdims=True)).astype(jnp.bfloat16)
    mixed_heads = jnp.einsum(
        "bhqk,bkhd->bqhd", weights, values_part, preferred_element_type=jnp.float32
    )
    part_blocks = blocks_here - 0
    mixed_rows = mixed_heads.reshape(part_blocks * BLK, feature_width)
    gate_rows = jnp.repeat(modulate[0:blocks_here, 2], BLK, axis=0)
    result = (stream + gate_rows * mixed_rows).astype(jnp.bfloat16)
    handed = from_behind(result[None], "segment", 1)
    return handed


def solution(mesh):
    placed = (
        P("segment", "frames", None),
        P("frames", None),
        P("segment", None, "frames"),
        P("segment", None, None, None),
        P("segment", "frames"),
        P("segment", "frames", None),
        P("segment", "frames"),
    )
    step = local
    if mesh.shape["frames"] == LINE * LANES * CORES:
        step = functools.partial(local_line, mesh.shape["segment"])
    return jax.shard_map(
        step, mesh=mesh, in_specs=placed, out_specs=P("segment", "frames", None), check_vma=False
    )
```

```python
import functools

import jax
import jax.numpy as jnp
from jax import lax
from jax.experimental import pallas as pl
from jax.experimental.pallas import tpu as pltpu
from jax.sharding import PartitionSpec as P

HEADS = 12
HD = 128
BLK = 64
MESH = pl.DeviceIdType.MESH
LINE, LANES, CORES = 4, 2, 2
GROUPS = 4
GH = HEADS // GROUPS
GW = GH * HD
PARTS = 2
NT_DIMS = (((1,), (1,)), ((), ()))


def tick_kernel(
    segs,
    hidden_ref, feat_ref, w_ref, mod_ref, ts_ref, list_ref, count_ref,
    out_ref,
    hbuf, mbuf, fbuf, wbuf, kv, qbuf, gbuf, res, qin, aout, ain, list_in, count_in,
    zsem, ysem, csem, rsem, osend, orecv, lsem, qsend, qrecv, asend, arecv,
):
    me = lax.axis_index("frames")
    seg = lax.axis_index("segment")
    c = me % CORES
    y = (me // CORES) % LANES
    z = me // (CORES * LANES)
    nxt = (seg + 1) % segs
    half = wbuf.shape[1]
    nblk = hidden_ref.shape[1] // BLK
    sel = list_ref.shape[2]
    part_rows = nblk * BLK // PARTS

    def shard(zz, yy, cc):
        return (zz * LANES + yy) * CORES + cc

    across = shard(z, 1 - y, c)

    def slot(p, s):
        return fbuf.at[s] if p == 0 else wbuf.at[2 * s + (p - 1)]

    def remote(src, dst, send, recv, **to):
        return pltpu.make_async_remote_copy(
            src_ref=src, dst_ref=dst, send_sem=send, recv_sem=recv,
            device_id=to, device_id_type=MESH,
        )

    def copy(p, s, to, sem):
        return remote(slot(p, s), slot(p, s), sem, rsem.at[p, s], frames=to)

    def z_copy(p, s, t, up):
        return copy(p, s, shard(z + 1 if up else z - 1, y, c), zsem.at[p, t, int(up)])

    def y_copy(zz):
        return copy(0, shard(zz, y, c), across, ysem.at[zz])

    def c_copy(p, zz, yy):
        return copy(p, shard(zz, yy, c), shard(z, y, 1 - c), csem.at[p, zz * LANES + yy])

    def wait_recv(p, s):
        copy(p, s, across, csem.at[0, 0]).wait_recv()

    def z_event(p, t):
        if t == 0:
            @pl.when(z > 0)
            def _():
                z_copy(p, me, 0, False).start()

            @pl.when(z < LINE - 1)
            def _():
                z_copy(p, me, 0, True).start()

            if p == 0:
                y_copy(z).start()
            c_copy(p, z, y).start()
            return

        @pl.when(z - t >= 0)
        def _():
            s = shard(z - t, y, c)
            wait_recv(p, s)

            @pl.when(z < LINE - 1)
            def _():
                z_copy(p, s, t, True).start()

            if p == 0:
                y_copy(z - t).start()
            c_copy(p, z - t, y).start()

        @pl.when(z + t <= LINE - 1)
        def _():
            s = shard(z + t, y, c)
            wait_recv(p, s)

            @pl.when(z > 0)
            def _():
                z_copy(p, s, t, False).start()

            if p == 0:
                y_copy(z + t).start()
            c_copy(p, z + t, y).start()

    def y_event(t):
        def arrive(zz):
            wait_recv(0, shard(zz, 1 - y, c))
            c_copy(0, zz, 1 - y).start()

        if t == 0:
            arrive(z)
            return

        @pl.when(z - t >= 0)
        def _():
            arrive(z - t)

        @pl.when(z + t <= LINE - 1)
        def _():
            arrive(z + t)

    def from_core(p, zz, yy):
        wait_recv(p, shard(zz, yy, 1 - c))

    def to_partner():
        return [
            remote(qbuf.at[2 * zz + 1 - y], qin.at[zz], qsend.at[zz], qrecv.at[zz], frames=across)
            for zz in range(2)
        ] + [
            remote(list_ref, list_in, qsend.at[2], qrecv.at[2], frames=across),
            remote(count_ref, count_in, qsend.at[3], qrecv.at[3], frames=across),
        ]

    def give_back(zz, i):
        rows = pl.ds(i * part_rows, part_rows)
        return remote(
            aout.at[zz, rows], ain.at[zz, rows], asend.at[zz, i], arecv.at[zz, i], frames=across
        )

    def hand(g, i):
        columns = pl.ds(pl.multiple_of(g * GW, GW), GW)
        rows = pl.ds(i * part_rows, part_rows)
        return remote(
            res.at[g, rows], out_ref.at[0, rows, columns], osend.at[g, i], orecv.at[g, i],
            segment=nxt,
        )

    def queries():
        def one(b, carry):
            rows = pl.ds(pl.multiple_of(b * BLK, BLK), BLK)
            x = hbuf[rows, :].astype(jnp.float32)
            normed = x * lax.rsqrt(jnp.mean(x * x, axis=-1, keepdims=True) + 1e-06)
            level = ts_ref[0, b]
            shift, scale, gate = (mbuf[i, level].reshape(1, -1) for i in range(3))
            q = (normed * (1.0 + scale) + shift).astype(jnp.bfloat16)
            for g in range(GROUPS):
                qbuf[g, rows, :] = q[:, g * GW:(g + 1) * GW]
                gbuf[g, b] = gate[:, g * GW:(g + 1) * GW]
            return carry

        lax.fori_loop(0, nblk, one, 0)

    def project(zz):
        weight = wbuf[pl.ds(2 * shard(zz, y, 0), 4)].reshape(4 * half, wbuf.shape[2])
        step = 4
        rows_step = step * fbuf.shape[1]

        def one(r, carry):
            f = fbuf[pl.ds(r * step, step)].reshape(rows_step, fbuf.shape[2])
            part = lax.dot_general(f, weight, NT_DIMS, preferred_element_type=jnp.float32)
            kv[zz, pl.ds(r * step, step)] = part.astype(jnp.bfloat16).reshape(step, BLK, GW)
            return carry

        lax.fori_loop(0, fbuf.shape[0] // step, one, 0)

    def attend(zz, b, q, blocks, counts):
        k = jnp.concatenate([kv[zz, blocks[0, b, j]] for j in range(sel)], axis=0)
        v = jnp.concatenate([kv[2 + zz, blocks[0, b, j]] for j in range(sel)], axis=0)
        live = lax.broadcasted_iota(jnp.int32, (BLK, sel * BLK), 1) < counts[0, b] * BLK
        mixed = []
        for h in range(GH):
            part = slice(h * HD, (h + 1) * HD)
            scores = lax.dot_general(
                q[:, part], k[:, part], NT_DIMS, preferred_element_type=jnp.float32
            )
            scores = jnp.where(live, scores * (1.0 / HD ** 0.5), jnp.float32(-1e30))
            expo = jnp.exp(scores - jnp.max(scores, axis=-1, keepdims=True))
            weights = (expo * (1.0 / jnp.sum(expo, axis=-1, keepdims=True))).astype(jnp.bfloat16)
            mixed.append(jnp.dot(weights, v[:, part], preferred_element_type=jnp.float32))
        return jnp.concatenate(mixed, axis=1)

    def finish(g, b, mixed):
        rows = slice(b * BLK, (b + 1) * BLK)
        columns = pl.ds(pl.multiple_of(g * GW, GW), GW)
        x = hbuf[rows, columns].astype(jnp.float32)
        res[g, rows, :] = (x + gbuf[g, b] * mixed).astype(jnp.bfloat16)

    def partner_rows(zz):
        for b in range(nblk):
            rows = slice(b * BLK, (b + 1) * BLK)
            mixed = attend(zz, b, qin[zz, rows, :], list_in, count_in)
            aout[zz, rows, :] = mixed.astype(jnp.bfloat16)
            if (b + 1) % (nblk // PARTS) == 0:
                give_back(zz, b // (nblk // PARTS)).start()

    def own_rows(zz):
        g = 2 * zz + y
        for b in range(nblk):
            rows = slice(b * BLK, (b + 1) * BLK)
            finish(g, b, attend(zz, b, qbuf[g, rows, :], list_ref, count_ref))
            if (b + 1) % (nblk // PARTS) == 0:
                hand(g, b // (nblk // PARTS)).start()

    def returned(zz):
        g = 2 * zz + 1 - y
        for b in range(nblk):
            if b % (nblk // PARTS) == 0:
                give_back(zz, b // (nblk // PARTS)).wait_recv()
            rows = slice(b * BLK, (b + 1) * BLK)
            finish(g, b, ain[zz, rows, :].astype(jnp.float32))
            if (b + 1) % (nblk // PARTS) == 0:
                hand(g, b // (nblk // PARTS)).start()

    loads = [
        pltpu.make_async_copy(src, dst, lsem.at[i])
        for i, (src, dst) in enumerate((
            (feat_ref, fbuf.at[me]),
            (w_ref.at[0, pl.ds(0, half)], wbuf.at[2 * me]),
            (w_ref.at[0, pl.ds(half, half)], wbuf.at[2 * me + 1]),
            (hidden_ref.at[0], hbuf),
            (mod_ref.at[0], mbuf),
        ))
    ]
    for load in loads:
        load.start()
    barrier = pltpu.get_barrier_semaphore()

    def greet(**where):
        pl.semaphore_signal(barrier, inc=1, device_id=where, device_id_type=MESH)

    @pl.when(z > 0)
    def _():
        greet(frames=shard(z - 1, y, c))

    @pl.when(z < LINE - 1)
    def _():
        greet(frames=shard(z + 1, y, c))

    greet(frames=across)
    greet(frames=shard(z, y, 1 - c))
    greet(segment=nxt)
    if segs > 2:
        greet(segment=(seg + segs - 1) % segs)
    ends = jnp.where(z == 0, 1, 0) + jnp.where(z == LINE - 1, 1, 0)
    pl.semaphore_wait(barrier, (5 if segs > 2 else 4) + 1 - ends)

    loads[0].wait()
    z_event(0, 0)
    loads[1].wait()
    z_event(1, 0)
    loads[2].wait()
    loads[3].wait()
    loads[4].wait()
    queries()
    z_event(0, 1)
    z_event(2, 0)
    for item in to_partner():
        item.start()
    z_event(0, 2)
    z_event(1, 1)
    z_event(2, 1)
    y_event(0)
    z_event(0, 3)
    y_event(1)
    y_event(2)
    z_event(1, 2)
    z_event(2, 2)
    y_event(3)
    for zz in range(LINE):
        for yy in range(LANES):
            from_core(0, zz, yy)

    def columns_in(zz):
        for p in (1, 2):
            from_core(p, zz, y)
        project(zz)

    order = (
        z,
        jnp.where(z == 0, 1, z - 1),
        jnp.where(z == 3, 1, jnp.where(z == 2, 3, 2)),
        jnp.where(z < 2, 3, 0),
    )
    first, other = z // 2, 1 - z // 2
    columns_in(order[0])
    columns_in(order[1])
    columns_in(order[2])
    z_event(1, 3)
    for item in to_partner():
        item.wait_recv()
    partner_rows(first)
    z_event(2, 3)
    own_rows(first)
    columns_in(order[3])
    partner_rows(other)
    own_rows(other)
    returned(first)
    returned(other)

    for p in range(3):
        for t in range(LINE - 1):
            @pl.when((z - t >= 0) & (z < LINE - 1))
            def _():
                z_copy(p, me, t, True).wait_send()

            @pl.when((z + t <= LINE - 1) & (z > 0))
            def _():
                z_copy(p, me, t, False).wait_send()

        for zz in range(LINE):
            c_copy(p, zz, y).wait_send()
    for zz in range(LINE):
        y_copy(zz).wait_send()
        c_copy(0, zz, 1 - y).wait_send()
    for item in to_partner():
        item.wait_send()
    for i in range(PARTS):
        for zz in range(2):
            give_back(zz, i).wait_send()
        for g in range(GROUPS):
            hand(g, i).wait()


def local_line(segs, hidden, features, kv_weight, mod_table, timestep, block_list, block_count):
    n = LINE * LANES * CORES
    rows, width = hidden.shape[1:]
    frows, fwidth = features.shape
    half = kv_weight.shape[2] // 2
    kv_weight = jnp.swapaxes(kv_weight, 1, 2)
    mod_table = jnp.swapaxes(mod_table, 1, 2)
    nblk = rows // BLK
    hbm = pl.BlockSpec(memory_space=pl.ANY)
    smem = pl.BlockSpec(memory_space=pltpu.SMEM)
    bf16 = jnp.bfloat16
    return pl.pallas_call(
        functools.partial(tick_kernel, segs),
        out_shape=jax.ShapeDtypeStruct(hidden.shape, bf16),
        in_specs=[hbm, hbm, hbm, hbm, smem, smem, smem],
        out_specs=hbm,
        scratch_shapes=[
            pltpu.VMEM((rows, width), bf16),
            pltpu.VMEM(mod_table.shape[1:], jnp.float32),
            pltpu.VMEM((n, frows, fwidth), bf16),
            pltpu.VMEM((2 * n, half, fwidth), bf16),
            pltpu.VMEM((GROUPS, n * frows // BLK, BLK, GW), bf16),
            pltpu.VMEM((GROUPS, rows, GW), bf16),
            pltpu.VMEM((GROUPS, nblk, 1, GW), jnp.float32),
            pltpu.VMEM((GROUPS, rows, GW), bf16),
            pltpu.VMEM((2, rows, GW), bf16),
            pltpu.VMEM((2, rows, GW), bf16),
            pltpu.VMEM((2, rows, GW), bf16),
            pltpu.SMEM(block_list.shape, jnp.int32),
            pltpu.SMEM(block_count.shape, jnp.int32),
            pltpu.SemaphoreType.DMA((3, LINE, 2)),
            pltpu.SemaphoreType.DMA((LINE,)),
            pltpu.SemaphoreType.DMA((3, LINE * LANES)),
            pltpu.SemaphoreType.DMA((3, n)),
            pltpu.SemaphoreType.DMA((GROUPS, PARTS)),
            pltpu.SemaphoreType.DMA((GROUPS, PARTS)),
            pltpu.SemaphoreType.DMA((5,)),
            pltpu.SemaphoreType.DMA((4,)),
            pltpu.SemaphoreType.DMA((4,)),
            pltpu.SemaphoreType.DMA((2, PARTS)),
            pltpu.SemaphoreType.DMA((2, PARTS)),
        ],
        compiler_params=pltpu.CompilerParams(
            collective_id=0, has_side_effects=True, vmem_limit_bytes=32 * 1024 * 1024
        ),
        cost_estimate=pl.CostEstimate(
            flops=2 * n * frows * fwidth * 2 * width, bytes_accessed=1 << 24,
            transcendentals=rows * 4 * BLK * HEADS,
        ),
    )(hidden, features, kv_weight, mod_table, timestep, block_list, block_count)


def from_behind(block, axis, distance):
    devices = range(lax.axis_size(axis))
    route = [((i - distance) % len(devices), i) for i in devices]
    return lax.ppermute(block, axis, route)


def local(hidden, features, kv_weight, mod_table, timestep, block_list, block_count):
    feature_table = lax.all_gather(features, "frames", axis=0, tiled=True)
    stream = hidden[0].astype(jnp.float32)
    tok_rows = stream.shape[0]
    feature_width = stream.shape[1]
    blocks_here = tok_rows // BLK
    normed = stream * lax.rsqrt(jnp.mean(stream * stream, axis=-1, keepdims=True) + 1e-06)
    levels = mod_table.shape[1]
    onehot = (timestep[0][:, None] == jnp.arange(levels, dtype=jnp.int32)[None, :]).astype(
        jnp.float32
    )
    modulate = jnp.sum(onehot[:, :, None, None] * mod_table[0][None], axis=1)
    normed_blocks = normed.reshape(blocks_here, BLK, feature_width)
    queries = (
        normed_blocks * (1.0 + modulate[:, 1][:, None, :]) + modulate[:, 0][:, None, :]
    ).astype(jnp.bfloat16)
    queries = queries.reshape(blocks_here, BLK, HEADS, HD)
    list_counts = block_count[0]
    list_blocks = block_list[0]
    slot_count = list_blocks.shape[1]
    offsets = jnp.arange(BLK, dtype=jnp.int32)
    inv_root = 1.0 / HD**0.5
    row_index = (list_blocks[:, :, None] * BLK + offsets[None, None, :]).reshape(-1)
    key_mask = jnp.repeat(
        jnp.arange(slot_count, dtype=jnp.int32)[None, :] < list_counts[:, None], BLK, axis=1
    )
    selected = jnp.take(feature_table, row_index, axis=0)
    key_values = jnp.dot(
        selected,
        lax.all_gather(kv_weight[0], "frames", axis=1, tiled=True),
        preferred_element_type=jnp.float32,
    ).astype(jnp.bfloat16)
    key_heads = key_values[:, :feature_width].reshape(-1, HEADS, HD)
    value_heads = key_values[:, feature_width:].reshape(-1, HEADS, HD)
    keys_part = key_heads.reshape(blocks_here, -1, HEADS, HD)
    values_part = value_heads.reshape(blocks_here, -1, HEADS, HD)
    scores = jnp.einsum("bqhd,bkhd->bhqk", queries, keys_part, preferred_element_type=jnp.float32)
    softmax_scores = scores
    softmax_scores = jnp.where(
        key_mask[:, None, None, :], softmax_scores * inv_root, jnp.float32(-1e30)
    )
    top_score = jnp.max(softmax_scores, axis=-1, keepdims=True)
    expo = jnp.exp(softmax_scores - top_score)
    weights = (expo / jnp.sum(expo, axis=-1, keepdims=True)).astype(jnp.bfloat16)
    mixed_heads = jnp.einsum(
        "bhqk,bkhd->bqhd", weights, values_part, preferred_element_type=jnp.float32
    )
    part_blocks = blocks_here - 0
    mixed_rows = mixed_heads.reshape(part_blocks * BLK, feature_width)
    gate_rows = jnp.repeat(modulate[0:blocks_here, 2], BLK, axis=0)
    result = (stream + gate_rows * mixed_rows).astype(jnp.bfloat16)
    handed = from_behind(result[None], "segment", 1)
    return handed


def solution(mesh):
    placed = (
        P("segment", "frames", None),
        P("frames", None),
        P("segment", None, "frames"),
        P("segment", None, None, None),
        P("segment", "frames"),
        P("segment", "frames", None),
        P("segment", "frames"),
    )
    step = local
    if mesh.shape["frames"] == LINE * LANES * CORES:
        step = functools.partial(local_line, mesh.shape["segment"])
    return jax.shard_map(
        step, mesh=mesh, in_specs=placed, out_specs=P("segment", "frames", None), check_vma=False
    )
```

```python
import functools

import jax
import jax.numpy as jnp
from jax import lax
from jax.experimental import pallas as pl
from jax.experimental.pallas import tpu as pltpu
from jax.sharding import PartitionSpec as P

HEADS = 12
HD = 128
BLK = 64
MESH = pl.DeviceIdType.MESH
LINE, LANES, CORES = 4, 2, 2
GROUPS = 4
GH = HEADS // GROUPS
GW = GH * HD
PARTS = 2
NT_DIMS = (((1,), (1,)), ((), ()))


def tick_kernel(
    segs,
    hidden_ref, feat_ref, w_ref, mod_ref, ts_ref, list_ref, count_ref,
    out_ref,
    hbuf, mbuf, fbuf, wbuf, kv, qbuf, gbuf, res, qin, aout, ain, list_in, count_in,
    zsem, ysem, csem, rsem, osend, orecv, lsem, qsend, qrecv, asend, arecv,
):
    me = lax.axis_index("frames")
    seg = lax.axis_index("segment")
    c = me % CORES
    y = (me // CORES) % LANES
    z = me // (CORES * LANES)
    nxt = (seg + 1) % segs
    half = wbuf.shape[1]
    nblk = hidden_ref.shape[1] // BLK
    sel = list_ref.shape[2]
    part_rows = nblk * BLK // PARTS

    def shard(zz, yy, cc):
        return (zz * LANES + yy) * CORES + cc

    across = shard(z, 1 - y, c)

    def slot(p, s):
        return fbuf.at[s] if p == 0 else wbuf.at[2 * s + (p - 1)]

    def remote(src, dst, send, recv, **to):
        return pltpu.make_async_remote_copy(
            src_ref=src, dst_ref=dst, send_sem=send, recv_sem=recv,
            device_id=to, device_id_type=MESH,
        )

    def copy(p, s, to, sem):
        return remote(slot(p, s), slot(p, s), sem, rsem.at[p, s], frames=to)

    def z_copy(p, s, t, up):
        return copy(p, s, shard(z + 1 if up else z - 1, y, c), zsem.at[p, t, int(up)])

    def y_copy(zz):
        return copy(0, shard(zz, y, c), across, ysem.at[zz])

    def c_copy(p, zz, yy):
        return copy(p, shard(zz, yy, c), shard(z, y, 1 - c), csem.at[p, zz * LANES + yy])

    def wait_recv(p, s):
        copy(p, s, across, csem.at[0, 0]).wait_recv()

    def spread(p, s, zz, t, downs, ups):
        def down():
            if downs is not False:
                @pl.when(downs)
                def _():
                    z_copy(p, s, t, False).start()

        def up():
            if ups is not False:
                @pl.when(ups)
                def _():
                    z_copy(p, s, t, True).start()

        def side():
            if p == 0:
                y_copy(zz).start()

        @pl.when(c == 0)
        def _():
            down()
            up()
            side()

        @pl.when(c == 1)
        def _():
            side()
            up()
            down()

        c_copy(p, zz, y).start()

    def z_event(p, t):
        if t == 0:
            spread(p, me, z, 0, z > 0, z < LINE - 1)
            return

        @pl.when(z - t >= 0)
        def _():
            s = shard(z - t, y, c)
            wait_recv(p, s)
            spread(p, s, z - t, t, False, z < LINE - 1)

        @pl.when(z + t <= LINE - 1)
        def _():
            s = shard(z + t, y, c)
            wait_recv(p, s)
            spread(p, s, z + t, t, z > 0, False)

    def y_event(t):
        def arrive(zz):
            wait_recv(0, shard(zz, 1 - y, c))
            c_copy(0, zz, 1 - y).start()

        if t == 0:
            arrive(z)
            return

        @pl.when(z - t >= 0)
        def _():
            arrive(z - t)

        @pl.when(z + t <= LINE - 1)
        def _():
            arrive(z + t)

    def from_core(p, zz, yy):
        wait_recv(p, shard(zz, yy, 1 - c))

    def to_partner():
        return [
            remote(qbuf.at[2 * zz + 1 - y], qin.at[zz], qsend.at[zz], qrecv.at[zz], frames=across)
            for zz in range(2)
        ] + [
            remote(list_ref, list_in, qsend.at[2], qrecv.at[2], frames=across),
            remote(count_ref, count_in, qsend.at[3], qrecv.at[3], frames=across),
        ]

    def give_back(zz, i):
        rows = pl.ds(i * part_rows, part_rows)
        return remote(
            aout.at[zz, rows], ain.at[zz, rows], asend.at[zz, i], arecv.at[zz, i], frames=across
        )

    def hand(g, i):
        columns = pl.ds(pl.multiple_of(g * GW, GW), GW)
        rows = pl.ds(i * part_rows, part_rows)
        return remote(
            res.at[g, rows], out_ref.at[0, rows, columns], osend.at[g, i], orecv.at[g, i],
            segment=nxt,
        )

    def queries(b):
        rows = slice(b * BLK, (b + 1) * BLK)
        x = hbuf[rows, :].astype(jnp.float32)
        normed = x * lax.rsqrt(jnp.mean(x * x, axis=-1, keepdims=True) + 1e-06)
        level = ts_ref[0, b]
        shift, scale, gate = (mbuf[i, level].reshape(1, -1) for i in range(3))
        q = (normed * (1.0 + scale) + shift).astype(jnp.bfloat16)
        for g in range(GROUPS):
            qbuf[g, rows, :] = q[:, g * GW:(g + 1) * GW]
            gbuf[g, b] = gate[:, g * GW:(g + 1) * GW]

    def project(zz):
        weight = wbuf[pl.ds(2 * shard(zz, y, 0), 4)].reshape(4 * half, wbuf.shape[2])
        step = 4
        rows_step = step * fbuf.shape[1]

        def one(r, carry):
            f = fbuf[pl.ds(r * step, step)].reshape(rows_step, fbuf.shape[2])
            part = lax.dot_general(f, weight, NT_DIMS, preferred_element_type=jnp.float32)
            kv[zz, pl.ds(r * step, step)] = part.astype(jnp.bfloat16).reshape(step, BLK, GW)
            return carry

        lax.fori_loop(0, fbuf.shape[0] // step, one, 0)

    def attend(zz, b, q, blocks, counts):
        k = jnp.concatenate([kv[zz, blocks[0, b, j]] for j in range(sel)], axis=0)
        v = jnp.concatenate([kv[2 + zz, blocks[0, b, j]] for j in range(sel)], axis=0)
        live = lax.broadcasted_iota(jnp.int32, (BLK, sel * BLK), 1) < counts[0, b] * BLK
        mixed = []
        for h in range(GH):
            part = slice(h * HD, (h + 1) * HD)
            scores = lax.dot_general(
                q[:, part], k[:, part], NT_DIMS, preferred_element_type=jnp.float32
            )
            scores = jnp.where(live, scores * (1.0 / HD ** 0.5), jnp.float32(-1e30))
            expo = jnp.exp(scores - jnp.max(scores, axis=-1, keepdims=True))
            weights = (expo * (1.0 / jnp.sum(expo, axis=-1, keepdims=True))).astype(jnp.bfloat16)
            mixed.append(jnp.dot(weights, v[:, part], preferred_element_type=jnp.float32))
        return jnp.concatenate(mixed, axis=1)

    def finish(g, b, mixed):
        rows = slice(b * BLK, (b + 1) * BLK)
        columns = pl.ds(pl.multiple_of(g * GW, GW), GW)
        x = hbuf[rows, columns].astype(jnp.float32)
        res[g, rows, :] = (x + gbuf[g, b] * mixed).astype(jnp.bfloat16)

    def partner_rows(zz):
        for b in range(nblk):
            rows = slice(b * BLK, (b + 1) * BLK)
            mixed = attend(zz, b, qin[zz, rows, :], list_in, count_in)
            aout[zz, rows, :] = mixed.astype(jnp.bfloat16)
            if (b + 1) % (nblk // PARTS) == 0:
                give_back(zz, b // (nblk // PARTS)).start()

    def own_rows(zz):
        g = 2 * zz + y
        for b in range(nblk):
            rows = slice(b * BLK, (b + 1) * BLK)
            finish(g, b, attend(zz, b, qbuf[g, rows, :], list_ref, count_ref))
            if (b + 1) % (nblk // PARTS) == 0:
                hand(g, b // (nblk // PARTS)).start()

    def returned(zz):
        g = 2 * zz + 1 - y
        for b in range(nblk):
            if b % (nblk // PARTS) == 0:
                give_back(zz, b // (nblk // PARTS)).wait_recv()
            rows = slice(b * BLK, (b + 1) * BLK)
            finish(g, b, ain[zz, rows, :].astype(jnp.float32))
            if (b + 1) % (nblk // PARTS) == 0:
                hand(g, b // (nblk // PARTS)).start()

    loads = [
        pltpu.make_async_copy(src, dst, lsem.at[i])
        for i, (src, dst) in enumerate((
            (feat_ref, fbuf.at[me]),
            (w_ref.at[0, pl.ds(0, half)], wbuf.at[2 * me]),
            (w_ref.at[0, pl.ds(half, half)], wbuf.at[2 * me + 1]),
            (hidden_ref.at[0], hbuf),
            (mod_ref.at[0], mbuf),
        ))
    ]
    for load in loads:
        load.start()
    barrier = pltpu.get_barrier_semaphore()

    def greet(**where):
        pl.semaphore_signal(barrier, inc=1, device_id=where, device_id_type=MESH)

    @pl.when(z > 0)
    def _():
        greet(frames=shard(z - 1, y, c))

    @pl.when(z < LINE - 1)
    def _():
        greet(frames=shard(z + 1, y, c))

    greet(frames=across)
    greet(frames=shard(z, y, 1 - c))
    greet(segment=nxt)
    if segs > 2:
        greet(segment=(seg + segs - 1) % segs)
    ends = jnp.where(z == 0, 1, 0) + jnp.where(z == LINE - 1, 1, 0)
    pl.semaphore_wait(barrier, (5 if segs > 2 else 4) + 1 - ends)

    loads[0].wait()
    z_event(0, 0)
    loads[1].wait()
    z_event(1, 0)
    loads[2].wait()
    loads[3].wait()
    loads[4].wait()
    z_event(0, 1)
    z_event(2, 0)
    queries(0)
    z_event(0, 2)
    z_event(1, 1)
    queries(1)
    z_event(2, 1)
    y_event(0)
    for b in range(2, nblk):
        queries(b)
    for item in to_partner():
        item.start()
    z_event(0, 3)
    y_event(1)
    y_event(2)
    z_event(1, 2)
    z_event(2, 2)
    y_event(3)
    for zz in range(LINE):
        for yy in range(LANES):
            from_core(0, zz, yy)

    def columns_in(zz):
        for p in (1, 2):
            from_core(p, zz, y)
        project(zz)

    order = (
        z,
        jnp.where(z == 0, 1, z - 1),
        jnp.where(z == 3, 1, jnp.where(z == 2, 3, 2)),
        jnp.where(z < 2, 3, 0),
    )
    first, other = z // 2, 1 - z // 2
    columns_in(order[0])
    columns_in(order[1])
    columns_in(order[2])
    z_event(1, 3)
    for item in to_partner():
        item.wait_recv()
    partner_rows(first)
    z_event(2, 3)
    own_rows(first)
    columns_in(order[3])
    partner_rows(other)
    own_rows(other)
    returned(first)
    returned(other)

    for p in range(3):
        for t in range(LINE - 1):
            @pl.when((z - t >= 0) & (z < LINE - 1))
            def _():
                z_copy(p, me, t, True).wait_send()

            @pl.when((z + t <= LINE - 1) & (z > 0))
            def _():
                z_copy(p, me, t, False).wait_send()

        for zz in range(LINE):
            c_copy(p, zz, y).wait_send()
    for zz in range(LINE):
        y_copy(zz).wait_send()
        c_copy(0, zz, 1 - y).wait_send()
    for item in to_partner():
        item.wait_send()
    for i in range(PARTS):
        for zz in range(2):
            give_back(zz, i).wait_send()
        for g in range(GROUPS):
            hand(g, i).wait()


def local_line(segs, hidden, features, kv_weight, mod_table, timestep, block_list, block_count):
    n = LINE * LANES * CORES
    rows, width = hidden.shape[1:]
    frows, fwidth = features.shape
    half = kv_weight.shape[2] // 2
    kv_weight = jnp.swapaxes(kv_weight, 1, 2)
    mod_table = jnp.swapaxes(mod_table, 1, 2)
    nblk = rows // BLK
    hbm = pl.BlockSpec(memory_space=pl.ANY)
    far = pl.BlockSpec(memory_space=pltpu.HBM)
    smem = pl.BlockSpec(memory_space=pltpu.SMEM)
    bf16 = jnp.bfloat16
    return pl.pallas_call(
        functools.partial(tick_kernel, segs),
        out_shape=jax.ShapeDtypeStruct(hidden.shape, bf16),
        in_specs=[far, far, far, far, smem, smem, smem],
        out_specs=hbm,
        scratch_shapes=[
            pltpu.VMEM((rows, width), bf16),
            pltpu.VMEM(mod_table.shape[1:], jnp.float32),
            pltpu.VMEM((n, frows, fwidth), bf16),
            pltpu.VMEM((2 * n, half, fwidth), bf16),
            pltpu.VMEM((GROUPS, n * frows // BLK, BLK, GW), bf16),
            pltpu.VMEM((GROUPS, rows, GW), bf16),
            pltpu.VMEM((GROUPS, nblk, 1, GW), jnp.float32),
            pltpu.VMEM((GROUPS, rows, GW), bf16),
            pltpu.VMEM((2, rows, GW), bf16),
            pltpu.VMEM((2, rows, GW), bf16),
            pltpu.VMEM((2, rows, GW), bf16),
            pltpu.SMEM(block_list.shape, jnp.int32),
            pltpu.SMEM(block_count.shape, jnp.int32),
            pltpu.SemaphoreType.DMA((3, LINE, 2)),
            pltpu.SemaphoreType.DMA((LINE,)),
            pltpu.SemaphoreType.DMA((3, LINE * LANES)),
            pltpu.SemaphoreType.DMA((3, n)),
            pltpu.SemaphoreType.DMA((GROUPS, PARTS)),
            pltpu.SemaphoreType.DMA((GROUPS, PARTS)),
            pltpu.SemaphoreType.DMA((5,)),
            pltpu.SemaphoreType.DMA((4,)),
            pltpu.SemaphoreType.DMA((4,)),
            pltpu.SemaphoreType.DMA((2, PARTS)),
            pltpu.SemaphoreType.DMA((2, PARTS)),
        ],
        compiler_params=pltpu.CompilerParams(
            collective_id=0, has_side_effects=True, vmem_limit_bytes=32 * 1024 * 1024
        ),
        cost_estimate=pl.CostEstimate(
            flops=2 * n * frows * fwidth * 2 * width, bytes_accessed=1 << 24,
            transcendentals=rows * 4 * BLK * HEADS,
        ),
    )(hidden, features, kv_weight, mod_table, timestep, block_list, block_count)


def from_behind(block, axis, distance):
    devices = range(lax.axis_size(axis))
    route = [((i - distance) % len(devices), i) for i in devices]
    return lax.ppermute(block, axis, route)


def local(hidden, features, kv_weight, mod_table, timestep, block_list, block_count):
    feature_table = lax.all_gather(features, "frames", axis=0, tiled=True)
    stream = hidden[0].astype(jnp.float32)
    tok_rows = stream.shape[0]
    feature_width = stream.shape[1]
    blocks_here = tok_rows // BLK
    normed = stream * lax.rsqrt(jnp.mean(stream * stream, axis=-1, keepdims=True) + 1e-06)
    levels = mod_table.shape[1]
    onehot = (timestep[0][:, None] == jnp.arange(levels, dtype=jnp.int32)[None, :]).astype(
        jnp.float32
    )
    modulate = jnp.sum(onehot[:, :, None, None] * mod_table[0][None], axis=1)
    normed_blocks = normed.reshape(blocks_here, BLK, feature_width)
    queries = (
        normed_blocks * (1.0 + modulate[:, 1][:, None, :]) + modulate[:, 0][:, None, :]
    ).astype(jnp.bfloat16)
    queries = queries.reshape(blocks_here, BLK, HEADS, HD)
    list_counts = block_count[0]
    list_blocks = block_list[0]
    slot_count = list_blocks.shape[1]
    offsets = jnp.arange(BLK, dtype=jnp.int32)
    inv_root = 1.0 / HD**0.5
    row_index = (list_blocks[:, :, None] * BLK + offsets[None, None, :]).reshape(-1)
    key_mask = jnp.repeat(
        jnp.arange(slot_count, dtype=jnp.int32)[None, :] < list_counts[:, None], BLK, axis=1
    )
    selected = jnp.take(feature_table, row_index, axis=0)
    key_values = jnp.dot(
        selected,
        lax.all_gather(kv_weight[0], "frames", axis=1, tiled=True),
        preferred_element_type=jnp.float32,
    ).astype(jnp.bfloat16)
    key_heads = key_values[:, :feature_width].reshape(-1, HEADS, HD)
    value_heads = key_values[:, feature_width:].reshape(-1, HEADS, HD)
    keys_part = key_heads.reshape(blocks_here, -1, HEADS, HD)
    values_part = value_heads.reshape(blocks_here, -1, HEADS, HD)
    scores = jnp.einsum("bqhd,bkhd->bhqk", queries, keys_part, preferred_element_type=jnp.float32)
    softmax_scores = scores
    softmax_scores = jnp.where(
        key_mask[:, None, None, :], softmax_scores * inv_root, jnp.float32(-1e30)
    )
    top_score = jnp.max(softmax_scores, axis=-1, keepdims=True)
    expo = jnp.exp(softmax_scores - top_score)
    weights = (expo / jnp.sum(expo, axis=-1, keepdims=True)).astype(jnp.bfloat16)
    mixed_heads = jnp.einsum(
        "bhqk,bkhd->bqhd", weights, values_part, preferred_element_type=jnp.float32
    )
    part_blocks = blocks_here - 0
    mixed_rows = mixed_heads.reshape(part_blocks * BLK, feature_width)
    gate_rows = jnp.repeat(modulate[0:blocks_here, 2], BLK, axis=0)
    result = (stream + gate_rows * mixed_rows).astype(jnp.bfloat16)
    handed = from_behind(result[None], "segment", 1)
    return handed


def solution(mesh):
    placed = (
        P("segment", "frames", None),
        P("frames", None),
        P("segment", None, "frames"),
        P("segment", None, None, None),
        P("segment", "frames"),
        P("segment", "frames", None),
        P("segment", "frames"),
    )
    step = local
    if mesh.shape["frames"] == LINE * LANES * CORES:
        step = functools.partial(local_line, mesh.shape["segment"])
    return jax.shard_map(
        step, mesh=mesh, in_specs=placed, out_specs=P("segment", "frames", None), check_vma=False
    )
```

```python
import functools

import jax
import jax.numpy as jnp
from jax import lax
from jax.experimental import pallas as pl
from jax.experimental.pallas import tpu as pltpu
from jax.sharding import PartitionSpec as P

HEADS = 12
HD = 128
BLK = 64
MESH = pl.DeviceIdType.MESH
LINE, LANES, CORES = 4, 2, 2
GROUPS = 4
GH = HEADS // GROUPS
GW = GH * HD
LIVE = 10
NT_DIMS = (((1,), (1,)), ((), ()))


def gather_kernel(
    segs,
    hidden_ref, feat_ref, w_ref, mod_ref, ts_ref, list_ref, count_ref,
    fbuf, wbuf, hin, min_, list_in, count_in,
    mst,
    zsem, ysem, csem, rsem, xsend, xrecv, lsem,
):
    me = lax.axis_index("frames")
    seg = lax.axis_index("segment")
    c = me % CORES
    y = (me // CORES) % LANES
    z = me // (CORES * LANES)
    nxt = (seg + 1) % segs
    half = wbuf.shape[1]
    nblk = mst.shape[0]

    def shard(zz, yy, cc):
        return (zz * LANES + yy) * CORES + cc

    across = shard(z, 1 - y, c)

    def slot(p, s):
        return fbuf.at[s] if p == 0 else wbuf.at[2 * s + (p - 1)]

    def remote(src, dst, send, recv, **to):
        return pltpu.make_async_remote_copy(
            src_ref=src, dst_ref=dst, send_sem=send, recv_sem=recv,
            device_id=to, device_id_type=MESH,
        )

    def copy(p, s, to, sem):
        return remote(slot(p, s), slot(p, s), sem, rsem.at[p, s], frames=to)

    def z_copy(p, s, t, up):
        return copy(p, s, shard(z + 1 if up else z - 1, y, c), zsem.at[p, t, int(up)])

    def y_copy(p, zz):
        return copy(p, shard(zz, y, c), across, ysem.at[p, zz])

    def c_copy(p, zz, yy):
        return copy(p, shard(zz, yy, c), shard(z, y, 1 - c), csem.at[p, zz * LANES + yy])

    def wait_recv(p, s):
        copy(p, s, across, csem.at[0, 0]).wait_recv()

    def hand_on():
        return [
            remote(w_ref.at[0, pl.ds(0, half)], wbuf.at[2 * me], xsend.at[0], rsem.at[1, me], segment=nxt),
            remote(w_ref.at[0, pl.ds(half, half)], wbuf.at[2 * me + 1], xsend.at[1], rsem.at[2, me], segment=nxt),
            remote(hidden_ref.at[0], hin, xsend.at[2], xrecv.at[2], segment=nxt),
            remote(list_ref, list_in, xsend.at[3], xrecv.at[3], segment=nxt),
            remote(count_ref, count_in, xsend.at[4], xrecv.at[4], segment=nxt),
            remote(mst, min_, xsend.at[5], xrecv.at[5], segment=nxt),
        ]

    def z_event(p, t):
        if t == 0:
            if p > 0:
                wait_recv(p, me)

            @pl.when(z > 0)
            def _():
                z_copy(p, me, 0, False).start()

            @pl.when(z < LINE - 1)
            def _():
                z_copy(p, me, 0, True).start()

            y_copy(p, z).start()
            c_copy(p, z, y).start()
            return

        @pl.when(z - t >= 0)
        def _():
            s = shard(z - t, y, c)
            wait_recv(p, s)

            @pl.when(z < LINE - 1)
            def _():
                z_copy(p, s, t, True).start()

            y_copy(p, z - t).start()
            c_copy(p, z - t, y).start()

        @pl.when(z + t <= LINE - 1)
        def _():
            s = shard(z + t, y, c)
            wait_recv(p, s)

            @pl.when(z > 0)
            def _():
                z_copy(p, s, t, False).start()

            y_copy(p, z + t).start()
            c_copy(p, z + t, y).start()

    def y_event(p, t):
        def arrive(zz):
            wait_recv(p, shard(zz, 1 - y, c))
            c_copy(p, zz, 1 - y).start()

        if t == 0:
            arrive(z)
            return

        @pl.when(z - t >= 0)
        def _():
            arrive(z - t)

        @pl.when(z + t <= LINE - 1)
        def _():
            arrive(z + t)

    load = pltpu.make_async_copy(feat_ref, fbuf.at[me], lsem)
    load.start()
    barrier = pltpu.get_barrier_semaphore()

    def greet(**where):
        pl.semaphore_signal(barrier, inc=1, device_id=where, device_id_type=MESH)

    @pl.when(z > 0)
    def _():
        greet(frames=shard(z - 1, y, c))

    @pl.when(z < LINE - 1)
    def _():
        greet(frames=shard(z + 1, y, c))

    greet(frames=across)
    greet(frames=shard(z, y, 1 - c))
    greet(segment=nxt)
    if segs > 2:
        greet(segment=(seg + segs - 1) % segs)
    for b in range(nblk):
        level = ts_ref[0, b]
        for i in range(3):
            mst[b, i:i + 1, :] = mod_ref[0, i, level].reshape(1, -1)
    ends = jnp.where(z == 0, 1, 0) + jnp.where(z == LINE - 1, 1, 0)
    pl.semaphore_wait(barrier, (5 if segs > 2 else 4) + 1 - ends)

    handed = hand_on()
    handed[0].start()
    handed[1].start()
    load.wait()
    z_event(0, 0)
    for item in handed[2:]:
        item.start()
    z_event(0, 1)
    z_event(1, 0)
    z_event(0, 2)
    z_event(2, 0)
    y_event(0, 0)
    z_event(1, 1)
    z_event(0, 3)
    y_event(0, 1)
    z_event(2, 1)
    y_event(1, 0)
    z_event(1, 2)
    y_event(0, 2)
    y_event(2, 0)
    z_event(2, 2)
    y_event(0, 3)
    y_event(1, 1)
    z_event(1, 3)
    y_event(2, 1)
    z_event(2, 3)
    y_event(1, 2)
    y_event(2, 2)
    y_event(1, 3)
    y_event(2, 3)
    for p in range(3):
        for zz in range(LINE):
            for yy in range(LANES):
                wait_recv(p, shard(zz, yy, 1 - c))
    for p in range(3):
        for t in range(LINE - 1):
            @pl.when((z - t >= 0) & (z < LINE - 1))
            def _():
                z_copy(p, me, t, True).wait_send()

            @pl.when((z + t <= LINE - 1) & (z > 0))
            def _():
                z_copy(p, me, t, False).wait_send()

        for zz in range(LINE):
            y_copy(p, zz).wait_send()
            for yy in range(LANES):
                c_copy(p, zz, yy).wait_send()
    for item in handed[:2]:
        item.wait_send()
    for item in handed[2:]:
        item.wait()


def attend_kernel(
    hidden_ref, mod_ref, f_ref, w_ref, list_ref, count_ref, out_ref, fsel, kv, qbuf
):
    rows = hidden_ref.shape[0]
    nblk = rows // BLK
    sel = list_ref.shape[2]
    width = hidden_ref.shape[1]
    counts = [count_ref[0, b] for b in range(nblk)]
    starts = [0]
    for b in range(nblk):
        starts.append(starts[-1] + counts[b])

    for b in range(nblk):
        for j in range(sel):
            @pl.when(j < counts[b])
            def _():
                fsel[starts[b] + j] = f_ref[list_ref[0, b, j]]

    per = kv.shape[0]
    wrows = w_ref.shape[1]
    tiles = w_ref.shape[0] // per
    features = fsel[...].reshape(fsel.shape[0] * BLK, fsel.shape[2])

    def project(i, carry):
        weight = w_ref[pl.ds(i * tiles, tiles)].reshape(tiles * wrows, w_ref.shape[2])
        part = lax.dot_general(features, weight, NT_DIMS, preferred_element_type=jnp.float32)
        kv[i] = part.astype(jnp.bfloat16).reshape(kv.shape[1:])
        return carry

    lax.fori_loop(0, per, project, 0)

    def block(b, start, live):
        span = pl.ds(pl.multiple_of(b * BLK, BLK), BLK)
        x = hidden_ref[span, :].astype(jnp.float32)
        normed = x * lax.rsqrt(jnp.mean(x * x, axis=-1, keepdims=True) + 1e-06)
        mod = mod_ref[b]
        qbuf[...] = (normed * (1.0 + mod[1:2]) + mod[0:1]).astype(jnp.bfloat16)

        def attend(n):
            for h in range(HEADS):
                g, part = h // GH, slice(h % GH * HD, (h % GH + 1) * HD)
                cols = slice(h * HD, (h + 1) * HD)
                k = kv[g, pl.ds(start, n), :, part].reshape(n * BLK, HD)
                v = kv[GROUPS + g, pl.ds(start, n), :, part].reshape(n * BLK, HD)
                scores = lax.dot_general(
                    qbuf[:, cols], k, NT_DIMS, preferred_element_type=jnp.float32
                ) * (1.0 / HD ** 0.5)
                expo = jnp.exp(scores - jnp.max(scores, axis=-1, keepdims=True))
                weights = (expo * (1.0 / jnp.sum(expo, axis=-1, keepdims=True))).astype(jnp.bfloat16)
                mixed = jnp.dot(weights, v, preferred_element_type=jnp.float32)
                out_ref[0, span, cols] = (
                    hidden_ref[span, cols].astype(jnp.float32) + mod[2:3, cols] * mixed
                ).astype(jnp.bfloat16)

        for n in range(1, sel + 1):
            @pl.when(live == n)
            def _():
                attend(n)

    def one(b, start):
        live = count_ref[0, b]
        block(b, start, live)
        return start + live

    lax.fori_loop(0, nblk, one, jnp.int32(0))


def local_line(segs, hidden, features, kv_weight, mod_table, timestep, block_list, block_count):
    n = LINE * LANES * CORES
    rows, width = hidden.shape[1:]
    frows, fwidth = features.shape
    half = kv_weight.shape[2] // 2
    nblk = rows // BLK
    hbm = pl.BlockSpec(memory_space=pl.ANY)
    vmem = pl.BlockSpec(memory_space=pltpu.VMEM)
    smem = pl.BlockSpec(memory_space=pltpu.SMEM)
    bf16 = jnp.bfloat16
    shape = jax.ShapeDtypeStruct
    table, weights, hin, mods, lists, counts = pl.pallas_call(
        functools.partial(gather_kernel, segs),
        out_shape=(
            shape((n, frows, fwidth), bf16),
            shape((2 * n, half, fwidth), bf16),
            shape((rows, width), bf16),
            shape((nblk, 3, width), jnp.float32),
            shape(block_list.shape, jnp.int32),
            shape(block_count.shape, jnp.int32),
        ),
        in_specs=[hbm, hbm, hbm, vmem, smem, smem, smem],
        out_specs=(hbm, hbm, hbm, hbm, smem, smem),
        scratch_shapes=[
            pltpu.VMEM((nblk, 3, width), jnp.float32),
            pltpu.SemaphoreType.DMA((3, LINE, 2)),
            pltpu.SemaphoreType.DMA((3, LINE)),
            pltpu.SemaphoreType.DMA((3, LINE * LANES)),
            pltpu.SemaphoreType.DMA((3, n)),
            pltpu.SemaphoreType.DMA((6,)),
            pltpu.SemaphoreType.DMA((6,)),
            pltpu.SemaphoreType.DMA,
        ],
        compiler_params=pltpu.CompilerParams(
            collective_id=0, has_side_effects=True, vmem_limit_bytes=16 * 1024 * 1024
        ),
        name="gather_kernel",
    )(
        hidden, features, jnp.swapaxes(kv_weight, 1, 2), jnp.swapaxes(mod_table, 1, 2),
        timestep, block_list, block_count,
    )
    return pl.pallas_call(
        attend_kernel,
        out_shape=shape(hidden.shape, bf16),
        in_specs=[vmem, vmem, vmem, vmem, smem, smem],
        out_specs=vmem,
        scratch_shapes=[
            pltpu.VMEM((LIVE, frows, fwidth), bf16),
            pltpu.VMEM((2 * GROUPS, LIVE, BLK, GW), bf16),
            pltpu.VMEM((BLK, width), bf16),
        ],
        compiler_params=pltpu.CompilerParams(vmem_limit_bytes=32 * 1024 * 1024),
        cost_estimate=pl.CostEstimate(
            flops=4 * LIVE * BLK * fwidth * width, bytes_accessed=1 << 23,
            transcendentals=LIVE * BLK * BLK * HEADS,
        ),
        name="attend_kernel",
    )(hin, mods, table, weights, lists, counts)


def from_behind(block, axis, distance):
    devices = range(lax.axis_size(axis))
    route = [((i - distance) % len(devices), i) for i in devices]
    return lax.ppermute(block, axis, route)


def local(hidden, features, kv_weight, mod_table, timestep, block_list, block_count):
    feature_table = lax.all_gather(features, "frames", axis=0, tiled=True)
    stream = hidden[0].astype(jnp.float32)
    tok_rows = stream.shape[0]
    feature_width = stream.shape[1]
    blocks_here = tok_rows // BLK
    normed = stream * lax.rsqrt(jnp.mean(stream * stream, axis=-1, keepdims=True) + 1e-06)
    levels = mod_table.shape[1]
    onehot = (timestep[0][:, None] == jnp.arange(levels, dtype=jnp.int32)[None, :]).astype(
        jnp.float32
    )
    modulate = jnp.sum(onehot[:, :, None, None] * mod_table[0][None], axis=1)
    normed_blocks = normed.reshape(blocks_here, BLK, feature_width)
    queries = (
        normed_blocks * (1.0 + modulate[:, 1][:, None, :]) + modulate[:, 0][:, None, :]
    ).astype(jnp.bfloat16)
    queries = queries.reshape(blocks_here, BLK, HEADS, HD)
    list_counts = block_count[0]
    list_blocks = block_list[0]
    slot_count = list_blocks.shape[1]
    offsets = jnp.arange(BLK, dtype=jnp.int32)
    inv_root = 1.0 / HD**0.5
    row_index = (list_blocks[:, :, None] * BLK + offsets[None, None, :]).reshape(-1)
    key_mask = jnp.repeat(
        jnp.arange(slot_count, dtype=jnp.int32)[None, :] < list_counts[:, None], BLK, axis=1
    )
    selected = jnp.take(feature_table, row_index, axis=0)
    key_values = jnp.dot(
        selected,
        lax.all_gather(kv_weight[0], "frames", axis=1, tiled=True),
        preferred_element_type=jnp.float32,
    ).astype(jnp.bfloat16)
    key_heads = key_values[:, :feature_width].reshape(-1, HEADS, HD)
    value_heads = key_values[:, feature_width:].reshape(-1, HEADS, HD)
    keys_part = key_heads.reshape(blocks_here, -1, HEADS, HD)
    values_part = value_heads.reshape(blocks_here, -1, HEADS, HD)
    scores = jnp.einsum("bqhd,bkhd->bhqk", queries, keys_part, preferred_element_type=jnp.float32)
    softmax_scores = scores
    softmax_scores = jnp.where(
        key_mask[:, None, None, :], softmax_scores * inv_root, jnp.float32(-1e30)
    )
    top_score = jnp.max(softmax_scores, axis=-1, keepdims=True)
    expo = jnp.exp(softmax_scores - top_score)
    weights = (expo / jnp.sum(expo, axis=-1, keepdims=True)).astype(jnp.bfloat16)
    mixed_heads = jnp.einsum(
        "bhqk,bkhd->bqhd", weights, values_part, preferred_element_type=jnp.float32
    )
    part_blocks = blocks_here - 0
    mixed_rows = mixed_heads.reshape(part_blocks * BLK, feature_width)
    gate_rows = jnp.repeat(modulate[0:blocks_here, 2], BLK, axis=0)
    result = (stream + gate_rows * mixed_rows).astype(jnp.bfloat16)
    handed = from_behind(result[None], "segment", 1)
    return handed


def solution(mesh):
    placed = (
        P("segment", "frames", None),
        P("frames", None),
        P("segment", None, "frames"),
        P("segment", None, None, None),
        P("segment", "frames"),
        P("segment", "frames", None),
        P("segment", "frames"),
    )
    step = local
    if mesh.shape["frames"] == LINE * LANES * CORES:
        step = functools.partial(local_line, mesh.shape["segment"])
    return jax.shard_map(
        step, mesh=mesh, in_specs=placed, out_specs=P("segment", "frames", None), check_vma=False
    )
```

```python
import functools

import jax
import jax.numpy as jnp
from jax import lax
from jax.experimental import pallas as pl
from jax.experimental.pallas import tpu as pltpu
from jax.sharding import PartitionSpec as P

HEADS = 12
HD = 128
BLK = 64
MESH = pl.DeviceIdType.MESH
LINE, LANES, CORES = 4, 2, 2
GROUPS = 4
GH = HEADS // GROUPS
GW = GH * HD
LIVE = 10
NT_DIMS = (((1,), (1,)), ((), ()))


def gather_kernel(
    segs,
    hidden_ref, feat_ref, w_ref, mod_ref, ts_ref, list_ref, count_ref,
    fbuf, wbuf, hin, min_, list_in, count_in,
    mst,
    zsem, ysem, csem, rsem, xsend, xrecv, lsem,
):
    me = lax.axis_index("frames")
    seg = lax.axis_index("segment")
    c = me % CORES
    y = (me // CORES) % LANES
    z = me // (CORES * LANES)
    nxt = (seg + 1) % segs
    half = wbuf.shape[1]
    nblk = mst.shape[0]

    def shard(zz, yy, cc):
        return (zz * LANES + yy) * CORES + cc

    across = shard(z, 1 - y, c)

    def slot(p, s):
        return fbuf.at[s] if p == 0 else wbuf.at[2 * s + (p - 1)]

    def remote(src, dst, send, recv, **to):
        return pltpu.make_async_remote_copy(
            src_ref=src, dst_ref=dst, send_sem=send, recv_sem=recv,
            device_id=to, device_id_type=MESH,
        )

    def copy(p, s, to, sem):
        return remote(slot(p, s), slot(p, s), sem, rsem.at[p, s], frames=to)

    def z_copy(p, s, t, up):
        return copy(p, s, shard(z + 1 if up else z - 1, y, c), zsem.at[p, t, int(up)])

    def y_copy(p, zz):
        return copy(p, shard(zz, y, c), across, ysem.at[p, zz])

    def c_copy(p, zz, yy):
        return copy(p, shard(zz, yy, c), shard(z, y, 1 - c), csem.at[p, zz * LANES + yy])

    def wait_recv(p, s):
        copy(p, s, across, csem.at[0, 0]).wait_recv()

    def hand_on():
        return [
            remote(w_ref.at[0, pl.ds(0, half)], wbuf.at[2 * me], xsend.at[0], rsem.at[1, me], segment=nxt),
            remote(w_ref.at[0, pl.ds(half, half)], wbuf.at[2 * me + 1], xsend.at[1], rsem.at[2, me], segment=nxt),
            remote(hidden_ref.at[0], hin, xsend.at[2], xrecv.at[2], segment=nxt),
            remote(list_ref, list_in, xsend.at[3], xrecv.at[3], segment=nxt),
            remote(count_ref, count_in, xsend.at[4], xrecv.at[4], segment=nxt),
            remote(mst, min_, xsend.at[5], xrecv.at[5], segment=nxt),
        ]

    def z_event(p, t):
        if t == 0:
            if p > 0:
                wait_recv(p, me)

            @pl.when(z > 0)
            def _():
                z_copy(p, me, 0, False).start()

            @pl.when(z < LINE - 1)
            def _():
                z_copy(p, me, 0, True).start()

            y_copy(p, z).start()
            c_copy(p, z, y).start()
            return

        @pl.when(z - t >= 0)
        def _():
            s = shard(z - t, y, c)
            wait_recv(p, s)

            @pl.when(z < LINE - 1)
            def _():
                z_copy(p, s, t, True).start()

            y_copy(p, z - t).start()
            c_copy(p, z - t, y).start()

        @pl.when(z + t <= LINE - 1)
        def _():
            s = shard(z + t, y, c)
            wait_recv(p, s)

            @pl.when(z > 0)
            def _():
                z_copy(p, s, t, False).start()

            y_copy(p, z + t).start()
            c_copy(p, z + t, y).start()

    def y_event(p, t):
        def arrive(zz):
            wait_recv(p, shard(zz, 1 - y, c))
            c_copy(p, zz, 1 - y).start()

        if t == 0:
            arrive(z)
            return

        @pl.when(z - t >= 0)
        def _():
            arrive(z - t)

        @pl.when(z + t <= LINE - 1)
        def _():
            arrive(z + t)

    load = pltpu.make_async_copy(feat_ref, fbuf.at[me], lsem)
    load.start()
    barrier = pltpu.get_barrier_semaphore()

    def greet(**where):
        pl.semaphore_signal(barrier, inc=1, device_id=where, device_id_type=MESH)

    @pl.when(z > 0)
    def _():
        greet(frames=shard(z - 1, y, c))

    @pl.when(z < LINE - 1)
    def _():
        greet(frames=shard(z + 1, y, c))

    greet(frames=across)
    greet(frames=shard(z, y, 1 - c))
    greet(segment=nxt)
    if segs > 2:
        greet(segment=(seg + segs - 1) % segs)
    for b in range(nblk):
        level = ts_ref[0, b]
        for i in range(3):
            mst[b, i:i + 1, :] = mod_ref[0, i, level].reshape(1, -1)
    ends = jnp.where(z == 0, 1, 0) + jnp.where(z == LINE - 1, 1, 0)
    pl.semaphore_wait(barrier, (5 if segs > 2 else 4) + 1 - ends)

    handed = hand_on()
    handed[0].start()
    handed[1].start()
    load.wait()
    z_event(0, 0)
    for item in handed[2:]:
        item.start()
    z_event(0, 1)
    z_event(1, 0)
    z_event(0, 2)
    z_event(2, 0)
    y_event(0, 0)
    z_event(1, 1)
    z_event(0, 3)
    y_event(0, 1)
    z_event(2, 1)
    y_event(1, 0)
    z_event(1, 2)
    y_event(0, 2)
    y_event(2, 0)
    z_event(2, 2)
    y_event(0, 3)
    y_event(1, 1)
    z_event(1, 3)
    y_event(2, 1)
    z_event(2, 3)
    y_event(1, 2)
    y_event(2, 2)
    y_event(1, 3)
    y_event(2, 3)
    for p in range(3):
        for zz in range(LINE):
            for yy in range(LANES):
                wait_recv(p, shard(zz, yy, 1 - c))
    for p in range(3):
        for t in range(LINE - 1):
            @pl.when((z - t >= 0) & (z < LINE - 1))
            def _():
                z_copy(p, me, t, True).wait_send()

            @pl.when((z + t <= LINE - 1) & (z > 0))
            def _():
                z_copy(p, me, t, False).wait_send()

        for zz in range(LINE):
            y_copy(p, zz).wait_send()
            for yy in range(LANES):
                c_copy(p, zz, yy).wait_send()
    for item in handed[:2]:
        item.wait_send()
    for item in handed[2:]:
        item.wait()


def attend_kernel(
    hidden_ref, mod_ref, f_ref, w_ref, list_ref, count_ref, out_ref, fsel, kv
):
    rows = hidden_ref.shape[0]
    nblk = rows // BLK
    sel = list_ref.shape[2]
    width = hidden_ref.shape[1]
    counts = [count_ref[0, b] for b in range(nblk)]
    starts = [0]
    for b in range(nblk):
        starts.append(starts[-1] + counts[b])

    for b in range(nblk):
        for j in range(sel):
            @pl.when(j < counts[b])
            def _():
                fsel[starts[b] + j] = f_ref[list_ref[0, b, j]]

    per = kv.shape[0]
    wrows = w_ref.shape[1]
    tiles = w_ref.shape[0] // per
    features = fsel[...].reshape(fsel.shape[0] * BLK, fsel.shape[2])

    def project(i, carry):
        weight = w_ref[pl.ds(i * tiles, tiles)].reshape(tiles * wrows, w_ref.shape[2])
        part = lax.dot_general(features, weight, NT_DIMS, preferred_element_type=jnp.float32)
        kv[i] = part.astype(jnp.bfloat16).reshape(kv.shape[1:])
        return carry

    lax.fori_loop(0, per, project, 0)

    def block(b, start, live):
        span = pl.ds(pl.multiple_of(b * BLK, BLK), BLK)
        x = hidden_ref[span, :].astype(jnp.float32)
        normed = x * lax.rsqrt(jnp.mean(x * x, axis=-1, keepdims=True) + 1e-06)
        mod = mod_ref[b]
        q = (normed * (1.0 + mod[1:2]) + mod[0:1]).astype(jnp.bfloat16)

        def attend(n):
            keys = [kv[g, pl.ds(start, n)].reshape(n * BLK, GW) for g in range(GROUPS)]
            values = [kv[GROUPS + g, pl.ds(start, n)].reshape(n * BLK, GW) for g in range(GROUPS)]
            parts = [(h // GH, slice(h % GH * HD, (h % GH + 1) * HD)) for h in range(HEADS)]
            scores = jnp.concatenate([
                lax.dot_general(
                    q[:, h * HD:(h + 1) * HD], keys[g][:, part], NT_DIMS,
                    preferred_element_type=jnp.float32,
                )
                for h, (g, part) in enumerate(parts)
            ], axis=0) * (1.0 / HD ** 0.5)
            expo = jnp.exp(scores - jnp.max(scores, axis=-1, keepdims=True))
            weights = (expo * (1.0 / jnp.sum(expo, axis=-1, keepdims=True))).astype(jnp.bfloat16)
            mixed = jnp.concatenate([
                jnp.dot(
                    weights[h * BLK:(h + 1) * BLK], values[g][:, part],
                    preferred_element_type=jnp.float32,
                )
                for h, (g, part) in enumerate(parts)
            ], axis=1)
            out_ref[0, span, :] = (
                hidden_ref[span, :].astype(jnp.float32) + mod[2:3] * mixed
            ).astype(jnp.bfloat16)

        for n in range(1, sel + 1):
            @pl.when(live == n)
            def _():
                attend(n)

    def one(b, start):
        live = count_ref[0, b]
        block(b, start, live)
        return start + live

    lax.fori_loop(0, nblk, one, jnp.int32(0))


def local_line(segs, hidden, features, kv_weight, mod_table, timestep, block_list, block_count):
    n = LINE * LANES * CORES
    rows, width = hidden.shape[1:]
    frows, fwidth = features.shape
    half = kv_weight.shape[2] // 2
    nblk = rows // BLK
    hbm = pl.BlockSpec(memory_space=pl.ANY)
    vmem = pl.BlockSpec(memory_space=pltpu.VMEM)
    smem = pl.BlockSpec(memory_space=pltpu.SMEM)
    bf16 = jnp.bfloat16
    shape = jax.ShapeDtypeStruct
    table, weights, hin, mods, lists, counts = pl.pallas_call(
        functools.partial(gather_kernel, segs),
        out_shape=(
            shape((n, frows, fwidth), bf16),
            shape((2 * n, half, fwidth), bf16),
            shape((rows, width), bf16),
            shape((nblk, 3, width), jnp.float32),
            shape(block_list.shape, jnp.int32),
            shape(block_count.shape, jnp.int32),
        ),
        in_specs=[vmem, vmem, vmem, vmem, smem, smem, smem],
        out_specs=(hbm, hbm, hbm, hbm, smem, smem),
        scratch_shapes=[
            pltpu.VMEM((nblk, 3, width), jnp.float32),
            pltpu.SemaphoreType.DMA((3, LINE, 2)),
            pltpu.SemaphoreType.DMA((3, LINE)),
            pltpu.SemaphoreType.DMA((3, LINE * LANES)),
            pltpu.SemaphoreType.DMA((3, n)),
            pltpu.SemaphoreType.DMA((6,)),
            pltpu.SemaphoreType.DMA((6,)),
            pltpu.SemaphoreType.DMA,
        ],
        compiler_params=pltpu.CompilerParams(
            collective_id=0, has_side_effects=True, vmem_limit_bytes=16 * 1024 * 1024
        ),
        name="gather_kernel",
    )(
        hidden, features, jnp.swapaxes(kv_weight, 1, 2), jnp.swapaxes(mod_table, 1, 2),
        timestep, block_list, block_count,
    )
    return pl.pallas_call(
        attend_kernel,
        out_shape=shape(hidden.shape, bf16),
        in_specs=[vmem, vmem, vmem, vmem, smem, smem],
        out_specs=vmem,
        scratch_shapes=[
            pltpu.VMEM((LIVE, frows, fwidth), bf16),
            pltpu.VMEM((2 * GROUPS, LIVE, BLK, GW), bf16),
        ],
        compiler_params=pltpu.CompilerParams(vmem_limit_bytes=32 * 1024 * 1024),
        cost_estimate=pl.CostEstimate(
            flops=4 * LIVE * BLK * fwidth * width, bytes_accessed=1 << 23,
            transcendentals=LIVE * BLK * BLK * HEADS,
        ),
        name="attend_kernel",
    )(hin, mods, table, weights, lists, counts)


def from_behind(block, axis, distance):
    devices = range(lax.axis_size(axis))
    route = [((i - distance) % len(devices), i) for i in devices]
    return lax.ppermute(block, axis, route)


def local(hidden, features, kv_weight, mod_table, timestep, block_list, block_count):
    feature_table = lax.all_gather(features, "frames", axis=0, tiled=True)
    stream = hidden[0].astype(jnp.float32)
    tok_rows = stream.shape[0]
    feature_width = stream.shape[1]
    blocks_here = tok_rows // BLK
    normed = stream * lax.rsqrt(jnp.mean(stream * stream, axis=-1, keepdims=True) + 1e-06)
    levels = mod_table.shape[1]
    onehot = (timestep[0][:, None] == jnp.arange(levels, dtype=jnp.int32)[None, :]).astype(
        jnp.float32
    )
    modulate = jnp.sum(onehot[:, :, None, None] * mod_table[0][None], axis=1)
    normed_blocks = normed.reshape(blocks_here, BLK, feature_width)
    queries = (
        normed_blocks * (1.0 + modulate[:, 1][:, None, :]) + modulate[:, 0][:, None, :]
    ).astype(jnp.bfloat16)
    queries = queries.reshape(blocks_here, BLK, HEADS, HD)
    list_counts = block_count[0]
    list_blocks = block_list[0]
    slot_count = list_blocks.shape[1]
    offsets = jnp.arange(BLK, dtype=jnp.int32)
    inv_root = 1.0 / HD**0.5
    row_index = (list_blocks[:, :, None] * BLK + offsets[None, None, :]).reshape(-1)
    key_mask = jnp.repeat(
        jnp.arange(slot_count, dtype=jnp.int32)[None, :] < list_counts[:, None], BLK, axis=1
    )
    selected = jnp.take(feature_table, row_index, axis=0)
    key_values = jnp.dot(
        selected,
        lax.all_gather(kv_weight[0], "frames", axis=1, tiled=True),
        preferred_element_type=jnp.float32,
    ).astype(jnp.bfloat16)
    key_heads = key_values[:, :feature_width].reshape(-1, HEADS, HD)
    value_heads = key_values[:, feature_width:].reshape(-1, HEADS, HD)
    keys_part = key_heads.reshape(blocks_here, -1, HEADS, HD)
    values_part = value_heads.reshape(blocks_here, -1, HEADS, HD)
    scores = jnp.einsum("bqhd,bkhd->bhqk", queries, keys_part, preferred_element_type=jnp.float32)
    softmax_scores = scores
    softmax_scores = jnp.where(
        key_mask[:, None, None, :], softmax_scores * inv_root, jnp.float32(-1e30)
    )
    top_score = jnp.max(softmax_scores, axis=-1, keepdims=True)
    expo = jnp.exp(softmax_scores - top_score)
    weights = (expo / jnp.sum(expo, axis=-1, keepdims=True)).astype(jnp.bfloat16)
    mixed_heads = jnp.einsum(
        "bhqk,bkhd->bqhd", weights, values_part, preferred_element_type=jnp.float32
    )
    part_blocks = blocks_here - 0
    mixed_rows = mixed_heads.reshape(part_blocks * BLK, feature_width)
    gate_rows = jnp.repeat(modulate[0:blocks_here, 2], BLK, axis=0)
    result = (stream + gate_rows * mixed_rows).astype(jnp.bfloat16)
    handed = from_behind(result[None], "segment", 1)
    return handed


def solution(mesh):
    placed = (
        P("segment", "frames", None),
        P("frames", None),
        P("segment", None, "frames"),
        P("segment", None, None, None),
        P("segment", "frames"),
        P("segment", "frames", None),
        P("segment", "frames"),
    )
    step = local
    if mesh.shape["frames"] == LINE * LANES * CORES:
        step = functools.partial(local_line, mesh.shape["segment"])
    return jax.shard_map(
        step, mesh=mesh, in_specs=placed, out_specs=P("segment", "frames", None), check_vma=False
    )
```

```python
import functools

import jax
import jax.numpy as jnp
from jax import lax
from jax.experimental import pallas as pl
from jax.experimental.pallas import tpu as pltpu
from jax.sharding import PartitionSpec as P

HEADS = 12
HD = 128
BLK = 64
MESH = pl.DeviceIdType.MESH
LINE, LANES, CORES = 4, 2, 2
GROUPS = 4
GH = HEADS // GROUPS
GW = GH * HD
LIVE = 10
NT_DIMS = (((1,), (1,)), ((), ()))


def gather_kernel(
    segs,
    hidden_ref, feat_ref, w_ref, mod_ref, ts_ref, list_ref, count_ref,
    kv_out, hin, min_, list_in, count_in,
    fbuf, wbuf, kv, mst, mbuf,
    zsem, ysem, csem, rsem, xsend, xrecv, lsem, ksem,
):
    me = lax.axis_index("frames")
    seg = lax.axis_index("segment")
    c = me % CORES
    y = (me // CORES) % LANES
    z = me // (CORES * LANES)
    nxt = (seg + 1) % segs
    half = wbuf.shape[1]
    nblk = mst.shape[0]

    def shard(zz, yy, cc):
        return (zz * LANES + yy) * CORES + cc

    across = shard(z, 1 - y, c)

    def slot(p, s):
        return fbuf.at[s] if p == 0 else wbuf.at[2 * s + (p - 1)]

    def remote(src, dst, send, recv, **to):
        return pltpu.make_async_remote_copy(
            src_ref=src, dst_ref=dst, send_sem=send, recv_sem=recv,
            device_id=to, device_id_type=MESH,
        )

    def copy(p, s, to, sem):
        return remote(slot(p, s), slot(p, s), sem, rsem.at[p, s], frames=to)

    def z_copy(p, s, t, up):
        return copy(p, s, shard(z + 1 if up else z - 1, y, c), zsem.at[p, t, int(up)])

    def y_copy(p, zz):
        return copy(p, shard(zz, y, c), across, ysem.at[p, zz])

    def c_copy(p, zz, yy):
        return copy(p, shard(zz, yy, c), shard(z, y, 1 - c), csem.at[p, zz * LANES + yy])

    def wait_recv(p, s):
        copy(p, s, across, csem.at[0, 0]).wait_recv()

    def hand_on():
        return [
            remote(w_ref.at[0, pl.ds(0, half)], wbuf.at[2 * me], xsend.at[0], rsem.at[1, me], segment=nxt),
            remote(w_ref.at[0, pl.ds(half, half)], wbuf.at[2 * me + 1], xsend.at[1], rsem.at[2, me], segment=nxt),
            remote(hidden_ref.at[0], hin, xsend.at[2], xrecv.at[2], segment=nxt),
            remote(list_ref, list_in, xsend.at[3], xrecv.at[3], segment=nxt),
            remote(count_ref, count_in, xsend.at[4], xrecv.at[4], segment=nxt),
            remote(mst, min_, xsend.at[5], xrecv.at[5], segment=nxt),
        ]

    def z_event(p, t):
        if t == 0:
            if p > 0:
                wait_recv(p, me)

            @pl.when(z > 0)
            def _():
                z_copy(p, me, 0, False).start()

            @pl.when(z < LINE - 1)
            def _():
                z_copy(p, me, 0, True).start()

            y_copy(p, z).start()
            c_copy(p, z, y).start()
            return

        @pl.when(z - t >= 0)
        def _():
            s = shard(z - t, y, c)
            wait_recv(p, s)

            @pl.when(z < LINE - 1)
            def _():
                z_copy(p, s, t, True).start()

            y_copy(p, z - t).start()
            c_copy(p, z - t, y).start()

        @pl.when(z + t <= LINE - 1)
        def _():
            s = shard(z + t, y, c)
            wait_recv(p, s)

            @pl.when(z > 0)
            def _():
                z_copy(p, s, t, False).start()

            y_copy(p, z + t).start()
            c_copy(p, z + t, y).start()

    def y_event(p, t):
        def arrive(zz):
            wait_recv(p, shard(zz, 1 - y, c))
            c_copy(p, zz, 1 - y).start()

        if t == 0:
            arrive(z)
            return

        @pl.when(z - t >= 0)
        def _():
            arrive(z - t)

        @pl.when(z + t <= LINE - 1)
        def _():
            arrive(z + t)

    def keep(zz, yy):
        pair = zz * LANES + yy
        return pltpu.make_async_copy(kv.at[pair], kv_out.at[pair], ksem.at[pair])

    def project(zz, yy):
        for p in (1, 2):
            wait_recv(p, shard(zz, yy, 1 - c))
        pair = zz * LANES + yy
        weight = wbuf[pl.ds(4 * pair, 4)].reshape(4 * half, wbuf.shape[2])
        step = fbuf.shape[0] // 2

        def one(r, carry):
            f = fbuf[pl.ds(r * step, step)].reshape(step * fbuf.shape[1], fbuf.shape[2])
            part = lax.dot_general(f, weight, NT_DIMS, preferred_element_type=jnp.float32)
            kv[pair, pl.ds(r * step, step)] = part.astype(jnp.bfloat16).reshape(step, BLK, GW)
            return carry

        lax.fori_loop(0, 2, one, 0)
        keep(zz, yy).start()

    load = pltpu.make_async_copy(feat_ref, fbuf.at[me], lsem.at[0])
    load.start()
    table = pltpu.make_async_copy(mod_ref.at[0], mbuf, lsem.at[1])
    table.start()
    barrier = pltpu.get_barrier_semaphore()

    def greet(**where):
        pl.semaphore_signal(barrier, inc=1, device_id=where, device_id_type=MESH)

    @pl.when(z > 0)
    def _():
        greet(frames=shard(z - 1, y, c))

    @pl.when(z < LINE - 1)
    def _():
        greet(frames=shard(z + 1, y, c))

    greet(frames=across)
    greet(frames=shard(z, y, 1 - c))
    greet(segment=nxt)
    if segs > 2:
        greet(segment=(seg + segs - 1) % segs)
    ends = jnp.where(z == 0, 1, 0) + jnp.where(z == LINE - 1, 1, 0)
    pl.semaphore_wait(barrier, (5 if segs > 2 else 4) + 1 - ends)

    handed = hand_on()
    handed[0].start()
    handed[1].start()
    load.wait()
    z_event(0, 0)
    for item in handed[2:5]:
        item.start()
    table.wait()
    for b in range(nblk):
        level = ts_ref[0, b]
        for i in range(3):
            mst[b, i:i + 1, :] = mbuf[i, level].reshape(1, -1)
    handed[5].start()
    z_event(0, 1)
    z_event(1, 0)
    z_event(0, 2)
    z_event(2, 0)
    y_event(0, 0)
    z_event(1, 1)
    z_event(0, 3)
    y_event(0, 1)
    z_event(2, 1)
    y_event(1, 0)
    z_event(1, 2)
    y_event(0, 2)
    y_event(2, 0)
    z_event(2, 2)
    y_event(0, 3)
    y_event(1, 1)
    for zz in range(LINE):
        for yy in range(LANES):
            wait_recv(0, shard(zz, yy, 1 - c))
    order = (
        z,
        jnp.where(z == 0, 1, z - 1),
        jnp.where(z == 3, 1, jnp.where(z == 2, 3, 2)),
        jnp.where(z < 2, 3, 0),
    )
    project(order[0], y)
    z_event(1, 3)
    y_event(2, 1)
    project(order[1], y)
    z_event(2, 3)
    project(order[0], 1 - y)
    y_event(1, 2)
    project(order[2], y)
    y_event(2, 2)
    project(order[1], 1 - y)
    y_event(1, 3)
    project(order[3], y)
    project(order[2], 1 - y)
    y_event(2, 3)
    project(order[3], 1 - y)
    for p in range(3):
        for t in range(LINE - 1):
            @pl.when((z - t >= 0) & (z < LINE - 1))
            def _():
                z_copy(p, me, t, True).wait_send()

            @pl.when((z + t <= LINE - 1) & (z > 0))
            def _():
                z_copy(p, me, t, False).wait_send()

        for zz in range(LINE):
            y_copy(p, zz).wait_send()
            for yy in range(LANES):
                c_copy(p, zz, yy).wait_send()
    for item in handed[:2]:
        item.wait_send()
    for item in handed[2:]:
        item.wait()
    for zz in range(LINE):
        for yy in range(LANES):
            keep(zz, yy).wait()


def attend_kernel(
    hidden_ref, mod_ref, kv_ref, list_ref, count_ref, out_ref, hbuf, mbuf, kv, qbuf, lsem, ksem
):
    rows = hbuf.shape[0]
    nblk = rows // BLK
    sel = list_ref.shape[2]

    def entry(b, j, at):
        return pltpu.make_async_copy(kv_ref.at[:, list_ref[0, b, j]], kv.at[:, at], ksem.at[at])

    loads = [
        pltpu.make_async_copy(hidden_ref, hbuf, lsem.at[0]),
        pltpu.make_async_copy(mod_ref, mbuf, lsem.at[1]),
    ]
    for load in loads:
        load.start()
    start = 0
    for b in range(nblk):
        live = count_ref[0, b]
        for j in range(sel):
            @pl.when(j < live)
            def _():
                entry(b, j, start + j).start()
        start = start + live
    for load in loads:
        load.wait()
    for b in range(nblk):
        span = slice(b * BLK, (b + 1) * BLK)
        x = hbuf[span, :].astype(jnp.float32)
        normed = x * lax.rsqrt(jnp.mean(x * x, axis=-1, keepdims=True) + 1e-06)
        mod = mbuf[b]
        qbuf[span, :] = (normed * (1.0 + mod[1:2]) + mod[0:1]).astype(jnp.bfloat16)

    def block(b, start, live):
        span = pl.ds(pl.multiple_of(b * BLK, BLK), BLK)
        q = qbuf[span, :]
        mod = mbuf[b]

        def attend(n):
            for j in range(n):
                entry(b, j, start + j).wait()
            keys = [kv[g, pl.ds(start, n)].reshape(n * BLK, GW) for g in range(GROUPS)]
            values = [kv[GROUPS + g, pl.ds(start, n)].reshape(n * BLK, GW) for g in range(GROUPS)]
            parts = [(h // GH, slice(h % GH * HD, (h % GH + 1) * HD)) for h in range(HEADS)]
            scores = jnp.concatenate([
                lax.dot_general(
                    q[:, h * HD:(h + 1) * HD], keys[g][:, part], NT_DIMS,
                    preferred_element_type=jnp.float32,
                )
                for h, (g, part) in enumerate(parts)
            ], axis=0) * (1.0 / HD ** 0.5)
            expo = jnp.exp(scores - jnp.max(scores, axis=-1, keepdims=True))
            weights = (expo * (1.0 / jnp.sum(expo, axis=-1, keepdims=True))).astype(jnp.bfloat16)
            mixed = jnp.concatenate([
                jnp.dot(
                    weights[h * BLK:(h + 1) * BLK], values[g][:, part],
                    preferred_element_type=jnp.float32,
                )
                for h, (g, part) in enumerate(parts)
            ], axis=1)
            out_ref[0, span, :] = (
                hbuf[span, :].astype(jnp.float32) + mod[2:3] * mixed
            ).astype(jnp.bfloat16)

        for n in range(1, sel + 1):
            @pl.when(live == n)
            def _():
                attend(n)

    def one(b, start):
        live = count_ref[0, b]
        block(b, start, live)
        return start + live

    lax.fori_loop(0, nblk, one, jnp.int32(0))


def local_line(segs, hidden, features, kv_weight, mod_table, timestep, block_list, block_count):
    n = LINE * LANES * CORES
    rows, width = hidden.shape[1:]
    frows, fwidth = features.shape
    half = kv_weight.shape[2] // 2
    nblk = rows // BLK
    hbm = pl.BlockSpec(memory_space=pl.ANY)
    vmem = pl.BlockSpec(memory_space=pltpu.VMEM)
    smem = pl.BlockSpec(memory_space=pltpu.SMEM)
    bf16 = jnp.bfloat16
    shape = jax.ShapeDtypeStruct
    kv_shape = (2 * GROUPS, n * frows // BLK, BLK, GW)
    limit = 60 * 1024 * 1024
    kv, hin, mods, lists, counts = pl.pallas_call(
        functools.partial(gather_kernel, segs),
        out_shape=(
            shape(kv_shape, bf16),
            shape((rows, width), bf16),
            shape((nblk, 3, width), jnp.float32),
            shape(block_list.shape, jnp.int32),
            shape(block_count.shape, jnp.int32),
        ),
        in_specs=[hbm, hbm, hbm, hbm, smem, smem, smem],
        out_specs=(hbm, hbm, hbm, smem, smem),
        scratch_shapes=[
            pltpu.VMEM((n, frows, fwidth), bf16),
            pltpu.VMEM((2 * n, half, fwidth), bf16),
            pltpu.VMEM(kv_shape, bf16),
            pltpu.VMEM((nblk, 3, width), jnp.float32),
            pltpu.VMEM((3, mod_table.shape[1], width), jnp.float32),
            pltpu.SemaphoreType.DMA((3, LINE, 2)),
            pltpu.SemaphoreType.DMA((3, LINE)),
            pltpu.SemaphoreType.DMA((3, LINE * LANES)),
            pltpu.SemaphoreType.DMA((3, n)),
            pltpu.SemaphoreType.DMA((6,)),
            pltpu.SemaphoreType.DMA((6,)),
            pltpu.SemaphoreType.DMA((2,)),
            pltpu.SemaphoreType.DMA((2 * GROUPS,)),
        ],
        compiler_params=pltpu.CompilerParams(
            collective_id=0, has_side_effects=True, vmem_limit_bytes=limit
        ),
        name="gather_kernel",
    )(
        hidden, features, jnp.swapaxes(kv_weight, 1, 2), jnp.swapaxes(mod_table, 1, 2),
        timestep, block_list, block_count,
    )
    return pl.pallas_call(
        attend_kernel,
        out_shape=shape(hidden.shape, bf16),
        in_specs=[hbm, hbm, hbm, smem, smem],
        out_specs=vmem,
        scratch_shapes=[
            pltpu.VMEM((rows, width), bf16),
            pltpu.VMEM((nblk, 3, width), jnp.float32),
            pltpu.VMEM((2 * GROUPS, LIVE, BLK, GW), bf16),
            pltpu.VMEM((rows, width), bf16),
            pltpu.SemaphoreType.DMA((2,)),
            pltpu.SemaphoreType.DMA((LIVE,)),
        ],
        compiler_params=pltpu.CompilerParams(vmem_limit_bytes=limit),
        cost_estimate=pl.CostEstimate(
            flops=4 * LIVE * BLK * BLK * width, bytes_accessed=1 << 22,
            transcendentals=LIVE * BLK * BLK * HEADS,
        ),
        name="attend_kernel",
    )(hin, mods, kv, lists, counts)


def from_behind(block, axis, distance):
    devices = range(lax.axis_size(axis))
    route = [((i - distance) % len(devices), i) for i in devices]
    return lax.ppermute(block, axis, route)


def local(hidden, features, kv_weight, mod_table, timestep, block_list, block_count):
    feature_table = lax.all_gather(features, "frames", axis=0, tiled=True)
    stream = hidden[0].astype(jnp.float32)
    tok_rows = stream.shape[0]
    feature_width = stream.shape[1]
    blocks_here = tok_rows // BLK
    normed = stream * lax.rsqrt(jnp.mean(stream * stream, axis=-1, keepdims=True) + 1e-06)
    levels = mod_table.shape[1]
    onehot = (timestep[0][:, None] == jnp.arange(levels, dtype=jnp.int32)[None, :]).astype(
        jnp.float32
    )
    modulate = jnp.sum(onehot[:, :, None, None] * mod_table[0][None], axis=1)
    normed_blocks = normed.reshape(blocks_here, BLK, feature_width)
    queries = (
        normed_blocks * (1.0 + modulate[:, 1][:, None, :]) + modulate[:, 0][:, None, :]
    ).astype(jnp.bfloat16)
    queries = queries.reshape(blocks_here, BLK, HEADS, HD)
    list_counts = block_count[0]
    list_blocks = block_list[0]
    slot_count = list_blocks.shape[1]
    offsets = jnp.arange(BLK, dtype=jnp.int32)
    inv_root = 1.0 / HD**0.5
    row_index = (list_blocks[:, :, None] * BLK + offsets[None, None, :]).reshape(-1)
    key_mask = jnp.repeat(
        jnp.arange(slot_count, dtype=jnp.int32)[None, :] < list_counts[:, None], BLK, axis=1
    )
    selected = jnp.take(feature_table, row_index, axis=0)
    key_values = jnp.dot(
        selected,
        lax.all_gather(kv_weight[0], "frames", axis=1, tiled=True),
        preferred_element_type=jnp.float32,
    ).astype(jnp.bfloat16)
    key_heads = key_values[:, :feature_width].reshape(-1, HEADS, HD)
    value_heads = key_values[:, feature_width:].reshape(-1, HEADS, HD)
    keys_part = key_heads.reshape(blocks_here, -1, HEADS, HD)
    values_part = value_heads.reshape(blocks_here, -1, HEADS, HD)
    scores = jnp.einsum("bqhd,bkhd->bhqk", queries, keys_part, preferred_element_type=jnp.float32)
    softmax_scores = scores
    softmax_scores = jnp.where(
        key_mask[:, None, None, :], softmax_scores * inv_root, jnp.float32(-1e30)
    )
    top_score = jnp.max(softmax_scores, axis=-1, keepdims=True)
    expo = jnp.exp(softmax_scores - top_score)
    weights = (expo / jnp.sum(expo, axis=-1, keepdims=True)).astype(jnp.bfloat16)
    mixed_heads = jnp.einsum(
        "bhqk,bkhd->bqhd", weights, values_part, preferred_element_type=jnp.float32
    )
    part_blocks = blocks_here - 0
    mixed_rows = mixed_heads.reshape(part_blocks * BLK, feature_width)
    gate_rows = jnp.repeat(modulate[0:blocks_here, 2], BLK, axis=0)
    result = (stream + gate_rows * mixed_rows).astype(jnp.bfloat16)
    handed = from_behind(result[None], "segment", 1)
    return handed


def solution(mesh):
    placed = (
        P("segment", "frames", None),
        P("frames", None),
        P("segment", None, "frames"),
        P("segment", None, None, None),
        P("segment", "frames"),
        P("segment", "frames", None),
        P("segment", "frames"),
    )
    step = local
    if mesh.shape["frames"] == LINE * LANES * CORES:
        step = functools.partial(local_line, mesh.shape["segment"])
    return jax.shard_map(
        step, mesh=mesh, in_specs=placed, out_specs=P("segment", "frames", None), check_vma=False
    )
```

```python
import functools

import jax
import jax.numpy as jnp
from jax import lax
from jax.experimental import pallas as pl
from jax.experimental.pallas import tpu as pltpu
from jax.sharding import PartitionSpec as P

HEADS = 12
HD = 128
BLK = 64
MESH = pl.DeviceIdType.MESH
LINE, LANES, CORES = 4, 2, 2
GROUPS = 4
GH = HEADS // GROUPS
GW = GH * HD
LIVE = 10
NT_DIMS = (((1,), (1,)), ((), ()))


def gather_kernel(
    segs,
    hidden_ref, feat_ref, w_ref, mod_ref, ts_ref, list_ref, count_ref,
    kv_out, hin, min_, list_in, count_in,
    fbuf, wbuf, kv, mst, mbuf,
    zsem, ysem, csem, rsem, xsend, xrecv, lsem, ksem, fsend, frecv,
):
    me = lax.axis_index("frames")
    seg = lax.axis_index("segment")
    c = me % CORES
    y = (me // CORES) % LANES
    z = me // (CORES * LANES)
    nxt = (seg + 1) % segs
    half = wbuf.shape[1]
    nblk = mst.shape[0]

    def shard(zz, yy, cc):
        return (zz * LANES + yy) * CORES + cc

    across = shard(z, 1 - y, c)

    def slot(p, s):
        return fbuf.at[s] if p == 0 else wbuf.at[2 * s + (p - 1)]

    def remote(src, dst, send, recv, **to):
        return pltpu.make_async_remote_copy(
            src_ref=src, dst_ref=dst, send_sem=send, recv_sem=recv,
            device_id=to, device_id_type=MESH,
        )

    def copy(p, s, to, sem):
        return remote(slot(p, s), slot(p, s), sem, rsem.at[p, s], frames=to)

    def z_copy(p, s, t, up):
        return copy(p, s, shard(z + 1 if up else z - 1, y, c), zsem.at[p, t, int(up)])

    def feature_half(s, part):
        rows = fbuf.shape[1] // 2
        return fbuf.at[s, pl.ds(pl.multiple_of(part * rows, rows), rows)]

    def y_copy(p, zz):
        s = shard(zz, y, c)
        if p > 0:
            return copy(p, s, across, ysem.at[p, zz])
        piece = feature_half(s, seg)
        return remote(piece, piece, ysem.at[p, zz], rsem.at[p, s], frames=across)

    def x_copy(zz):
        piece = feature_half(shard(zz, 1 - y, c), seg)
        return remote(piece, piece, fsend.at[zz], frecv.at[zz], segment=nxt)

    def c_copy(p, zz, yy):
        return copy(p, shard(zz, yy, c), shard(z, y, 1 - c), csem.at[p, zz * LANES + yy])

    def wait_recv(p, s):
        copy(p, s, across, csem.at[0, 0]).wait_recv()

    def hand_on():
        first = hin.shape[0] // 2
        return [
            remote(w_ref.at[0, pl.ds(0, half)], wbuf.at[2 * me], xsend.at[0], rsem.at[1, me], segment=nxt),
            remote(w_ref.at[0, pl.ds(half, half)], wbuf.at[2 * me + 1], xsend.at[1], rsem.at[2, me], segment=nxt),
            remote(
                hidden_ref.at[0, pl.ds(0, first)], hin.at[pl.ds(0, first)],
                xsend.at[2], xrecv.at[2], segment=nxt,
            ),
            remote(list_ref, list_in, xsend.at[3], xrecv.at[3], segment=nxt),
            remote(count_ref, count_in, xsend.at[4], xrecv.at[4], segment=nxt),
            remote(mst, min_, xsend.at[5], xrecv.at[5], segment=nxt),
            remote(
                hidden_ref.at[0, pl.ds(first, first)], hin.at[pl.ds(first, first)],
                xsend.at[6], xrecv.at[6], segment=nxt,
            ),
        ]

    def z_event(p, t):
        if t == 0:
            if p > 0:
                wait_recv(p, me)

            @pl.when(z > 0)
            def _():
                z_copy(p, me, 0, False).start()

            @pl.when(z < LINE - 1)
            def _():
                z_copy(p, me, 0, True).start()

            y_copy(p, z).start()
            c_copy(p, z, y).start()
            return

        @pl.when(z - t >= 0)
        def _():
            s = shard(z - t, y, c)
            wait_recv(p, s)

            @pl.when(z < LINE - 1)
            def _():
                z_copy(p, s, t, True).start()

            y_copy(p, z - t).start()
            c_copy(p, z - t, y).start()

        @pl.when(z + t <= LINE - 1)
        def _():
            s = shard(z + t, y, c)
            wait_recv(p, s)

            @pl.when(z > 0)
            def _():
                z_copy(p, s, t, False).start()

            y_copy(p, z + t).start()
            c_copy(p, z + t, y).start()

    def y_event(p, t):
        def arrive(zz):
            s = shard(zz, 1 - y, c)
            if p > 0:
                wait_recv(p, s)
                c_copy(p, zz, 1 - y).start()
                return
            piece = feature_half(s, seg)
            remote(piece, piece, fsend.at[zz], rsem.at[p, s], frames=across).wait_recv()
            x_copy(zz).start()

        at_distance(t, arrive)

    def x_event(t):
        def arrive(zz):
            x_copy(zz).wait_recv()
            c_copy(0, zz, 1 - y).start()

        at_distance(t, arrive)

    def at_distance(t, arrive):
        if t == 0:
            arrive(z)
            return

        @pl.when(z - t >= 0)
        def _():
            arrive(z - t)

        @pl.when(z + t <= LINE - 1)
        def _():
            arrive(z + t)

    def keep(zz, yy):
        pair = zz * LANES + yy
        return pltpu.make_async_copy(kv.at[pair], kv_out.at[pair], ksem.at[pair])

    def project(zz, yy):
        for p in (1, 2):
            wait_recv(p, shard(zz, yy, 1 - c))
        pair = zz * LANES + yy
        weight = wbuf[pl.ds(4 * pair, 4)].reshape(4 * half, wbuf.shape[2])
        step = fbuf.shape[0] // 2

        def one(r, carry):
            f = fbuf[pl.ds(r * step, step)].reshape(step * fbuf.shape[1], fbuf.shape[2])
            part = lax.dot_general(f, weight, NT_DIMS, preferred_element_type=jnp.float32)
            kv[pair, pl.ds(r * step, step)] = part.astype(jnp.bfloat16).reshape(step, BLK, GW)
            return carry

        lax.fori_loop(0, 2, one, 0)
        keep(zz, yy).start()

    load = pltpu.make_async_copy(feat_ref, fbuf.at[me], lsem.at[0])
    load.start()
    table = pltpu.make_async_copy(mod_ref.at[0], mbuf, lsem.at[1])
    table.start()
    barrier = pltpu.get_barrier_semaphore()

    def greet(**where):
        pl.semaphore_signal(barrier, inc=1, device_id=where, device_id_type=MESH)

    @pl.when(z > 0)
    def _():
        greet(frames=shard(z - 1, y, c))

    @pl.when(z < LINE - 1)
    def _():
        greet(frames=shard(z + 1, y, c))

    greet(frames=across)
    greet(frames=shard(z, y, 1 - c))
    greet(segment=nxt)
    if segs > 2:
        greet(segment=(seg + segs - 1) % segs)
    ends = jnp.where(z == 0, 1, 0) + jnp.where(z == LINE - 1, 1, 0)
    pl.semaphore_wait(barrier, (5 if segs > 2 else 4) + 1 - ends)

    handed = hand_on()
    handed[0].start()
    handed[1].start()
    load.wait()
    z_event(0, 0)
    for item in handed[2:5]:
        item.start()
    table.wait()
    for b in range(nblk):
        level = ts_ref[0, b]
        for i in range(3):
            mst[b, i:i + 1, :] = mbuf[i, level].reshape(1, -1)
    handed[5].start()
    z_event(0, 1)
    z_event(1, 0)
    z_event(0, 2)
    z_event(2, 0)
    y_event(0, 0)
    z_event(1, 1)
    y_event(0, 1)
    z_event(0, 3)
    z_event(2, 1)
    y_event(0, 2)
    z_event(1, 2)
    y_event(1, 0)
    y_event(0, 3)
    handed[6].start()
    z_event(2, 2)
    x_event(0)
    x_event(1)
    y_event(2, 0)
    x_event(2)
    x_event(3)
    y_event(1, 1)
    for zz in range(LINE):
        for yy in range(LANES):
            wait_recv(0, shard(zz, yy, 1 - c))
    order = (
        z,
        jnp.where(z == 0, 1, z - 1),
        jnp.where(z == 3, 1, jnp.where(z == 2, 3, 2)),
        jnp.where(z < 2, 3, 0),
    )
    project(order[0], y)
    z_event(1, 3)
    y_event(2, 1)
    project(order[1], y)
    z_event(2, 3)
    project(order[0], 1 - y)
    y_event(1, 2)
    project(order[2], y)
    y_event(2, 2)
    project(order[1], 1 - y)
    y_event(1, 3)
    project(order[3], y)
    project(order[2], 1 - y)
    y_event(2, 3)
    project(order[3], 1 - y)
    for p in range(3):
        for t in range(LINE - 1):
            @pl.when((z - t >= 0) & (z < LINE - 1))
            def _():
                z_copy(p, me, t, True).wait_send()

            @pl.when((z + t <= LINE - 1) & (z > 0))
            def _():
                z_copy(p, me, t, False).wait_send()

        for zz in range(LINE):
            y_copy(p, zz).wait_send()
            for yy in range(LANES):
                c_copy(p, zz, yy).wait_send()
    for zz in range(LINE):
        x_copy(zz).wait_send()
    for item in handed[:2]:
        item.wait_send()
    for item in handed[2:]:
        item.wait()
    for zz in range(LINE):
        for yy in range(LANES):
            keep(zz, yy).wait()


def attend_kernel(
    hidden_ref, mod_ref, kv_ref, list_ref, count_ref, out_ref, hbuf, mbuf, kv, qbuf, lsem, ksem
):
    rows = hbuf.shape[0]
    nblk = rows // BLK
    sel = list_ref.shape[2]

    def entry(b, j, at):
        return pltpu.make_async_copy(kv_ref.at[:, list_ref[0, b, j]], kv.at[:, at], ksem.at[at])

    loads = [
        pltpu.make_async_copy(hidden_ref, hbuf, lsem.at[0]),
        pltpu.make_async_copy(mod_ref, mbuf, lsem.at[1]),
    ]
    for load in loads:
        load.start()
    start = 0
    for b in range(nblk):
        live = count_ref[0, b]
        for j in range(sel):
            @pl.when(j < live)
            def _():
                entry(b, j, start + j).start()
        start = start + live
    for load in loads:
        load.wait()
    for b in range(nblk):
        span = slice(b * BLK, (b + 1) * BLK)
        x = hbuf[span, :].astype(jnp.float32)
        normed = x * lax.rsqrt(jnp.mean(x * x, axis=-1, keepdims=True) + 1e-06)
        mod = mbuf[b]
        qbuf[span, :] = (normed * (1.0 + mod[1:2]) + mod[0:1]).astype(jnp.bfloat16)

    def block(b, start, live):
        span = pl.ds(pl.multiple_of(b * BLK, BLK), BLK)
        q = qbuf[span, :]
        mod = mbuf[b]

        def attend(n):
            for j in range(n):
                entry(b, j, start + j).wait()
            keys = [kv[g, pl.ds(start, n)].reshape(n * BLK, GW) for g in range(GROUPS)]
            values = [kv[GROUPS + g, pl.ds(start, n)].reshape(n * BLK, GW) for g in range(GROUPS)]
            parts = [(h // GH, slice(h % GH * HD, (h % GH + 1) * HD)) for h in range(HEADS)]
            scores = jnp.concatenate([
                lax.dot_general(
                    q[:, h * HD:(h + 1) * HD], keys[g][:, part], NT_DIMS,
                    preferred_element_type=jnp.float32,
                )
                for h, (g, part) in enumerate(parts)
            ], axis=0) * (1.0 / HD ** 0.5)
            expo = jnp.exp(scores - jnp.max(scores, axis=-1, keepdims=True))
            weights = (expo * (1.0 / jnp.sum(expo, axis=-1, keepdims=True))).astype(jnp.bfloat16)
            mixed = jnp.concatenate([
                jnp.dot(
                    weights[h * BLK:(h + 1) * BLK], values[g][:, part],
                    preferred_element_type=jnp.float32,
                )
                for h, (g, part) in enumerate(parts)
            ], axis=1)
            out_ref[0, span, :] = (
                hbuf[span, :].astype(jnp.float32) + mod[2:3] * mixed
            ).astype(jnp.bfloat16)

        for n in range(1, sel + 1):
            @pl.when(live == n)
            def _():
                attend(n)

    def one(b, start):
        live = count_ref[0, b]
        block(b, start, live)
        return start + live

    lax.fori_loop(0, nblk, one, jnp.int32(0))


def local_line(segs, hidden, features, kv_weight, mod_table, timestep, block_list, block_count):
    n = LINE * LANES * CORES
    rows, width = hidden.shape[1:]
    frows, fwidth = features.shape
    half = kv_weight.shape[2] // 2
    nblk = rows // BLK
    hbm = pl.BlockSpec(memory_space=pl.ANY)
    vmem = pl.BlockSpec(memory_space=pltpu.VMEM)
    smem = pl.BlockSpec(memory_space=pltpu.SMEM)
    bf16 = jnp.bfloat16
    shape = jax.ShapeDtypeStruct
    kv_shape = (2 * GROUPS, n * frows // BLK, BLK, GW)
    limit = 60 * 1024 * 1024
    kv, hin, mods, lists, counts = pl.pallas_call(
        functools.partial(gather_kernel, segs),
        out_shape=(
            shape(kv_shape, bf16),
            shape((rows, width), bf16),
            shape((nblk, 3, width), jnp.float32),
            shape(block_list.shape, jnp.int32),
            shape(block_count.shape, jnp.int32),
        ),
        in_specs=[hbm, hbm, hbm, hbm, smem, smem, smem],
        out_specs=(hbm, hbm, hbm, smem, smem),
        scratch_shapes=[
            pltpu.VMEM((n, frows, fwidth), bf16),
            pltpu.VMEM((2 * n, half, fwidth), bf16),
            pltpu.VMEM(kv_shape, bf16),
            pltpu.VMEM((nblk, 3, width), jnp.float32),
            pltpu.VMEM((3, mod_table.shape[1], width), jnp.float32),
            pltpu.SemaphoreType.DMA((3, LINE, 2)),
            pltpu.SemaphoreType.DMA((3, LINE)),
            pltpu.SemaphoreType.DMA((3, LINE * LANES)),
            pltpu.SemaphoreType.DMA((3, n)),
            pltpu.SemaphoreType.DMA((7,)),
            pltpu.SemaphoreType.DMA((7,)),
            pltpu.SemaphoreType.DMA((2,)),
            pltpu.SemaphoreType.DMA((2 * GROUPS,)),
            pltpu.SemaphoreType.DMA((LINE,)),
            pltpu.SemaphoreType.DMA((LINE,)),
        ],
        compiler_params=pltpu.CompilerParams(
            collective_id=0, has_side_effects=True, vmem_limit_bytes=limit
        ),
        name="gather_kernel",
    )(
        hidden, features, jnp.swapaxes(kv_weight, 1, 2), jnp.swapaxes(mod_table, 1, 2),
        timestep, block_list, block_count,
    )
    return pl.pallas_call(
        attend_kernel,
        out_shape=shape(hidden.shape, bf16),
        in_specs=[hbm, hbm, hbm, smem, smem],
        out_specs=vmem,
        scratch_shapes=[
            pltpu.VMEM((rows, width), bf16),
            pltpu.VMEM((nblk, 3, width), jnp.float32),
            pltpu.VMEM((2 * GROUPS, LIVE, BLK, GW), bf16),
            pltpu.VMEM((rows, width), bf16),
            pltpu.SemaphoreType.DMA((2,)),
            pltpu.SemaphoreType.DMA((LIVE,)),
        ],
        compiler_params=pltpu.CompilerParams(vmem_limit_bytes=limit),
        cost_estimate=pl.CostEstimate(
            flops=4 * LIVE * BLK * BLK * width, bytes_accessed=1 << 22,
            transcendentals=LIVE * BLK * BLK * HEADS,
        ),
        name="attend_kernel",
    )(hin, mods, kv, lists, counts)


def from_behind(block, axis, distance):
    devices = range(lax.axis_size(axis))
    route = [((i - distance) % len(devices), i) for i in devices]
    return lax.ppermute(block, axis, route)


def local(hidden, features, kv_weight, mod_table, timestep, block_list, block_count):
    feature_table = lax.all_gather(features, "frames", axis=0, tiled=True)
    stream = hidden[0].astype(jnp.float32)
    tok_rows = stream.shape[0]
    feature_width = stream.shape[1]
    blocks_here = tok_rows // BLK
    normed = stream * lax.rsqrt(jnp.mean(stream * stream, axis=-1, keepdims=True) + 1e-06)
    levels = mod_table.shape[1]
    onehot = (timestep[0][:, None] == jnp.arange(levels, dtype=jnp.int32)[None, :]).astype(
        jnp.float32
    )
    modulate = jnp.sum(onehot[:, :, None, None] * mod_table[0][None], axis=1)
    normed_blocks = normed.reshape(blocks_here, BLK, feature_width)
    queries = (
        normed_blocks * (1.0 + modulate[:, 1][:, None, :]) + modulate[:, 0][:, None, :]
    ).astype(jnp.bfloat16)
    queries = queries.reshape(blocks_here, BLK, HEADS, HD)
    list_counts = block_count[0]
    list_blocks = block_list[0]
    slot_count = list_blocks.shape[1]
    offsets = jnp.arange(BLK, dtype=jnp.int32)
    inv_root = 1.0 / HD**0.5
    row_index = (list_blocks[:, :, None] * BLK + offsets[None, None, :]).reshape(-1)
    key_mask = jnp.repeat(
        jnp.arange(slot_count, dtype=jnp.int32)[None, :] < list_counts[:, None], BLK, axis=1
    )
    selected = jnp.take(feature_table, row_index, axis=0)
    key_values = jnp.dot(
        selected,
        lax.all_gather(kv_weight[0], "frames", axis=1, tiled=True),
        preferred_element_type=jnp.float32,
    ).astype(jnp.bfloat16)
    key_heads = key_values[:, :feature_width].reshape(-1, HEADS, HD)
    value_heads = key_values[:, feature_width:].reshape(-1, HEADS, HD)
    keys_part = key_heads.reshape(blocks_here, -1, HEADS, HD)
    values_part = value_heads.reshape(blocks_here, -1, HEADS, HD)
    scores = jnp.einsum("bqhd,bkhd->bhqk", queries, keys_part, preferred_element_type=jnp.float32)
    softmax_scores = scores
    softmax_scores = jnp.where(
        key_mask[:, None, None, :], softmax_scores * inv_root, jnp.float32(-1e30)
    )
    top_score = jnp.max(softmax_scores, axis=-1, keepdims=True)
    expo = jnp.exp(softmax_scores - top_score)
    weights = (expo / jnp.sum(expo, axis=-1, keepdims=True)).astype(jnp.bfloat16)
    mixed_heads = jnp.einsum(
        "bhqk,bkhd->bqhd", weights, values_part, preferred_element_type=jnp.float32
    )
    part_blocks = blocks_here - 0
    mixed_rows = mixed_heads.reshape(part_blocks * BLK, feature_width)
    gate_rows = jnp.repeat(modulate[0:blocks_here, 2], BLK, axis=0)
    result = (stream + gate_rows * mixed_rows).astype(jnp.bfloat16)
    handed = from_behind(result[None], "segment", 1)
    return handed


def solution(mesh):
    placed = (
        P("segment", "frames", None),
        P("frames", None),
        P("segment", None, "frames"),
        P("segment", None, None, None),
        P("segment", "frames"),
        P("segment", "frames", None),
        P("segment", "frames"),
    )
    step = local
    if mesh.shape["frames"] == LINE * LANES * CORES and mesh.shape["segment"] == 2:
        step = functools.partial(local_line, mesh.shape["segment"])
    return jax.shard_map(
        step, mesh=mesh, in_specs=placed, out_specs=P("segment", "frames", None), check_vma=False
    )
```

```python
import functools

import jax
import jax.numpy as jnp
from jax import lax
from jax.experimental import pallas as pl
from jax.experimental.pallas import tpu as pltpu
from jax.sharding import PartitionSpec as P

HEADS = 12
HD = 128
BLK = 64
MESH = pl.DeviceIdType.MESH
LINE, LANES, CORES = 4, 2, 2
GROUPS = 4
PIECES = 4
GH = HEADS // GROUPS
GW = GH * HD
LIVE = 10
NT_DIMS = (((1,), (1,)), ((), ()))


def gather_kernel(
    segs,
    hidden_ref, feat_ref, w_ref, mod_ref, ts_ref, list_ref, count_ref,
    kv_out, hin, min_, list_in, count_in,
    fbuf, wbuf, kv, mst, mbuf,
    zsem, ysem, csem, rsem, xsend, xrecv, lsem, ksem, fsend, frecv, wsend,
):
    me = lax.axis_index("frames")
    seg = lax.axis_index("segment")
    c = me % CORES
    y = (me // CORES) % LANES
    z = me // (CORES * LANES)
    nxt = (seg + 1) % segs
    piece = wbuf.shape[1]
    nblk = mst.shape[0]

    def shard(zz, yy, cc):
        return (zz * LANES + yy) * CORES + cc

    across = shard(z, 1 - y, c)

    def slot(p, s):
        return fbuf.at[s] if p == 0 else wbuf.at[PIECES * s + (p - 1)]

    def remote(src, dst, send, recv, **to):
        return pltpu.make_async_remote_copy(
            src_ref=src, dst_ref=dst, send_sem=send, recv_sem=recv,
            device_id=to, device_id_type=MESH,
        )

    def copy(p, s, to, sem):
        return remote(slot(p, s), slot(p, s), sem, rsem.at[p, s], frames=to)

    def z_copy(p, s, t, up):
        return copy(p, s, shard(z + 1 if up else z - 1, y, c), zsem.at[p, t, int(up)])

    def feature_half(s, part):
        rows = fbuf.shape[1] // 2
        return fbuf.at[s, pl.ds(pl.multiple_of(part * rows, rows), rows)]

    def y_copy(p, zz):
        s = shard(zz, y, c)
        if p > 0:
            return copy(p, s, across, ysem.at[p, zz])
        part = feature_half(s, seg)
        return remote(part, part, ysem.at[p, zz], rsem.at[p, s], frames=across)

    def x_copy(zz):
        part = feature_half(shard(zz, 1 - y, c), seg)
        return remote(part, part, fsend.at[zz], frecv.at[zz], segment=nxt)

    def c_copy(p, zz, yy):
        return copy(p, shard(zz, yy, c), shard(z, y, 1 - c), csem.at[p, zz * LANES + yy])

    def wait_recv(p, s):
        copy(p, s, across, csem.at[0, 0]).wait_recv()

    def hand_on():
        first = hin.shape[0] // 2
        return [
            remote(
                w_ref.at[0, pl.ds(i * piece, piece)], wbuf.at[PIECES * me + i],
                wsend.at[i], rsem.at[1 + i, me], segment=nxt,
            )
            for i in range(PIECES)
        ], [
            remote(
                hidden_ref.at[0, pl.ds(0, first)], hin.at[pl.ds(0, first)],
                xsend.at[0], xrecv.at[0], segment=nxt,
            ),
            remote(list_ref, list_in, xsend.at[1], xrecv.at[1], segment=nxt),
            remote(count_ref, count_in, xsend.at[2], xrecv.at[2], segment=nxt),
            remote(mst, min_, xsend.at[3], xrecv.at[3], segment=nxt),
            remote(
                hidden_ref.at[0, pl.ds(first, first)], hin.at[pl.ds(first, first)],
                xsend.at[4], xrecv.at[4], segment=nxt,
            ),
        ]

    def z_event(p, t):
        if t == 0:
            if p > 0:
                wait_recv(p, me)

            @pl.when(z > 0)
            def _():
                z_copy(p, me, 0, False).start()

            @pl.when(z < LINE - 1)
            def _():
                z_copy(p, me, 0, True).start()

            y_copy(p, z).start()
            c_copy(p, z, y).start()
            return

        @pl.when(z - t >= 0)
        def _():
            s = shard(z - t, y, c)
            wait_recv(p, s)

            @pl.when(z < LINE - 1)
            def _():
                z_copy(p, s, t, True).start()

            y_copy(p, z - t).start()
            c_copy(p, z - t, y).start()

        @pl.when(z + t <= LINE - 1)
        def _():
            s = shard(z + t, y, c)
            wait_recv(p, s)

            @pl.when(z > 0)
            def _():
                z_copy(p, s, t, False).start()

            y_copy(p, z + t).start()
            c_copy(p, z + t, y).start()

    def y_event(p, t):
        def arrive(zz):
            s = shard(zz, 1 - y, c)
            if p > 0:
                wait_recv(p, s)
                c_copy(p, zz, 1 - y).start()
                return
            part = feature_half(s, seg)
            remote(part, part, fsend.at[zz], rsem.at[p, s], frames=across).wait_recv()
            x_copy(zz).start()

        at_distance(t, arrive)

    def x_event(t):
        def arrive(zz):
            x_copy(zz).wait_recv()
            c_copy(0, zz, 1 - y).start()

        at_distance(t, arrive)

    def at_distance(t, arrive):
        if t == 0:
            arrive(z)
            return

        @pl.when(z - t >= 0)
        def _():
            arrive(z - t)

        @pl.when(z + t <= LINE - 1)
        def _():
            arrive(z + t)

    def keep(zz, yy):
        pair = zz * LANES + yy
        return pltpu.make_async_copy(kv.at[pair], kv_out.at[pair], ksem.at[pair])

    def project(zz, yy):
        for p in range(1, 1 + PIECES):
            wait_recv(p, shard(zz, yy, 1 - c))
        pair = zz * LANES + yy
        both = CORES * PIECES
        weight = wbuf[pl.ds(both * pair, both)].reshape(both * piece, wbuf.shape[2])
        step = fbuf.shape[0] // 2

        def one(r, carry):
            f = fbuf[pl.ds(r * step, step)].reshape(step * fbuf.shape[1], fbuf.shape[2])
            part = lax.dot_general(f, weight, NT_DIMS, preferred_element_type=jnp.float32)
            kv[pair, pl.ds(r * step, step)] = part.astype(jnp.bfloat16).reshape(step, BLK, GW)
            return carry

        lax.fori_loop(0, 2, one, 0)
        keep(zz, yy).start()

    load = pltpu.make_async_copy(feat_ref, fbuf.at[me], lsem.at[0])
    load.start()
    table = pltpu.make_async_copy(mod_ref.at[0], mbuf, lsem.at[1])
    table.start()
    barrier = pltpu.get_barrier_semaphore()

    def greet(**where):
        pl.semaphore_signal(barrier, inc=1, device_id=where, device_id_type=MESH)

    @pl.when(z > 0)
    def _():
        greet(frames=shard(z - 1, y, c))

    @pl.when(z < LINE - 1)
    def _():
        greet(frames=shard(z + 1, y, c))

    greet(frames=across)
    greet(frames=shard(z, y, 1 - c))
    greet(segment=nxt)
    if segs > 2:
        greet(segment=(seg + segs - 1) % segs)
    ends = jnp.where(z == 0, 1, 0) + jnp.where(z == LINE - 1, 1, 0)
    pl.semaphore_wait(barrier, (5 if segs > 2 else 4) + 1 - ends)

    columns, handed = hand_on()
    for item in columns:
        item.start()
    load.wait()
    z_event(0, 0)
    for item in handed[1:3]:
        item.start()
    table.wait()
    for b in range(nblk):
        level = ts_ref[0, b]
        for i in range(3):
            mst[b, i:i + 1, :] = mbuf[i, level].reshape(1, -1)
    handed[3].start()
    z_event(0, 1)
    z_event(1, 0)
    z_event(2, 0)
    z_event(0, 2)
    z_event(3, 0)
    z_event(4, 0)
    y_event(0, 0)
    z_event(1, 1)
    z_event(2, 1)
    y_event(0, 1)
    z_event(0, 3)
    z_event(3, 1)
    z_event(4, 1)
    y_event(0, 2)
    z_event(1, 2)
    z_event(2, 2)
    y_event(1, 0)
    y_event(2, 0)
    y_event(0, 3)
    handed[0].start()
    handed[4].start()
    z_event(3, 2)
    z_event(4, 2)
    x_event(0)
    x_event(1)
    y_event(3, 0)
    y_event(4, 0)
    x_event(2)
    x_event(3)
    y_event(1, 1)
    y_event(2, 1)
    for zz in range(LINE):
        for yy in range(LANES):
            wait_recv(0, shard(zz, yy, 1 - c))
    order = (
        z,
        jnp.where(z == 0, 1, z - 1),
        jnp.where(z == 3, 1, jnp.where(z == 2, 3, 2)),
        jnp.where(z < 2, 3, 0),
    )
    project(order[0], y)
    z_event(1, 3)
    z_event(2, 3)
    y_event(3, 1)
    y_event(4, 1)
    project(order[1], y)
    z_event(3, 3)
    z_event(4, 3)
    project(order[0], 1 - y)
    y_event(1, 2)
    y_event(2, 2)
    project(order[2], y)
    y_event(3, 2)
    y_event(4, 2)
    project(order[1], 1 - y)
    y_event(1, 3)
    y_event(2, 3)
    project(order[3], y)
    project(order[2], 1 - y)
    y_event(3, 3)
    y_event(4, 3)
    project(order[3], 1 - y)
    for p in range(1 + PIECES):
        for t in range(LINE - 1):
            @pl.when((z - t >= 0) & (z < LINE - 1))
            def _():
                z_copy(p, me, t, True).wait_send()

            @pl.when((z + t <= LINE - 1) & (z > 0))
            def _():
                z_copy(p, me, t, False).wait_send()

        for zz in range(LINE):
            y_copy(p, zz).wait_send()
            for yy in range(LANES):
                c_copy(p, zz, yy).wait_send()
    for zz in range(LINE):
        x_copy(zz).wait_send()
    for item in columns:
        item.wait_send()
    for item in handed:
        item.wait()
    for zz in range(LINE):
        for yy in range(LANES):
            keep(zz, yy).wait()


def attend_kernel(
    hidden_ref, mod_ref, kv_ref, list_ref, count_ref, out_ref, hbuf, mbuf, kv, qbuf, lsem, ksem
):
    rows = hbuf.shape[0]
    nblk = rows // BLK
    sel = list_ref.shape[2]

    def entry(b, j, at):
        return pltpu.make_async_copy(kv_ref.at[:, list_ref[0, b, j]], kv.at[:, at], ksem.at[at])

    loads = [
        pltpu.make_async_copy(hidden_ref, hbuf, lsem.at[0]),
        pltpu.make_async_copy(mod_ref, mbuf, lsem.at[1]),
    ]
    for load in loads:
        load.start()
    start = 0
    for b in range(nblk):
        live = count_ref[0, b]
        for j in range(sel):
            @pl.when(j < live)
            def _():
                entry(b, j, start + j).start()
        start = start + live
    for load in loads:
        load.wait()
    for b in range(nblk):
        span = slice(b * BLK, (b + 1) * BLK)
        x = hbuf[span, :].astype(jnp.float32)
        normed = x * lax.rsqrt(jnp.mean(x * x, axis=-1, keepdims=True) + 1e-06)
        mod = mbuf[b]
        qbuf[span, :] = (normed * (1.0 + mod[1:2]) + mod[0:1]).astype(jnp.bfloat16)

    def block(b, start, live):
        span = pl.ds(pl.multiple_of(b * BLK, BLK), BLK)
        q = qbuf[span, :]
        mod = mbuf[b]

        def attend(n):
            for j in range(n):
                entry(b, j, start + j).wait()
            keys = [kv[g, pl.ds(start, n)].reshape(n * BLK, GW) for g in range(GROUPS)]
            values = [kv[GROUPS + g, pl.ds(start, n)].reshape(n * BLK, GW) for g in range(GROUPS)]
            parts = [(h // GH, slice(h % GH * HD, (h % GH + 1) * HD)) for h in range(HEADS)]
            scores = jnp.concatenate([
                lax.dot_general(
                    q[:, h * HD:(h + 1) * HD], keys[g][:, part], NT_DIMS,
                    preferred_element_type=jnp.float32,
                )
                for h, (g, part) in enumerate(parts)
            ], axis=0) * (1.0 / HD ** 0.5)
            expo = jnp.exp(scores - jnp.max(scores, axis=-1, keepdims=True))
            weights = (expo * (1.0 / jnp.sum(expo, axis=-1, keepdims=True))).astype(jnp.bfloat16)
            mixed = jnp.concatenate([
                jnp.dot(
                    weights[h * BLK:(h + 1) * BLK], values[g][:, part],
                    preferred_element_type=jnp.float32,
                )
                for h, (g, part) in enumerate(parts)
            ], axis=1)
            out_ref[0, span, :] = (
                hbuf[span, :].astype(jnp.float32) + mod[2:3] * mixed
            ).astype(jnp.bfloat16)

        for n in range(1, sel + 1):
            @pl.when(live == n)
            def _():
                attend(n)

    def one(b, start):
        live = count_ref[0, b]
        block(b, start, live)
        return start + live

    lax.fori_loop(0, nblk, one, jnp.int32(0))


def local_line(segs, hidden, features, kv_weight, mod_table, timestep, block_list, block_count):
    n = LINE * LANES * CORES
    rows, width = hidden.shape[1:]
    frows, fwidth = features.shape
    piece = kv_weight.shape[2] // PIECES
    nblk = rows // BLK
    hbm = pl.BlockSpec(memory_space=pl.ANY)
    vmem = pl.BlockSpec(memory_space=pltpu.VMEM)
    smem = pl.BlockSpec(memory_space=pltpu.SMEM)
    bf16 = jnp.bfloat16
    shape = jax.ShapeDtypeStruct
    kv_shape = (2 * GROUPS, n * frows // BLK, BLK, GW)
    limit = 60 * 1024 * 1024
    kv, hin, mods, lists, counts = pl.pallas_call(
        functools.partial(gather_kernel, segs),
        out_shape=(
            shape(kv_shape, bf16),
            shape((rows, width), bf16),
            shape((nblk, 3, width), jnp.float32),
            shape(block_list.shape, jnp.int32),
            shape(block_count.shape, jnp.int32),
        ),
        in_specs=[hbm, hbm, hbm, hbm, smem, smem, smem],
        out_specs=(hbm, hbm, hbm, smem, smem),
        scratch_shapes=[
            pltpu.VMEM((n, frows, fwidth), bf16),
            pltpu.VMEM((PIECES * n, piece, fwidth), bf16),
            pltpu.VMEM(kv_shape, bf16),
            pltpu.VMEM((nblk, 3, width), jnp.float32),
            pltpu.VMEM((3, mod_table.shape[1], width), jnp.float32),
            pltpu.SemaphoreType.DMA((1 + PIECES, LINE, 2)),
            pltpu.SemaphoreType.DMA((1 + PIECES, LINE)),
            pltpu.SemaphoreType.DMA((1 + PIECES, LINE * LANES)),
            pltpu.SemaphoreType.DMA((1 + PIECES, n)),
            pltpu.SemaphoreType.DMA((5,)),
            pltpu.SemaphoreType.DMA((5,)),
            pltpu.SemaphoreType.DMA((2,)),
            pltpu.SemaphoreType.DMA((2 * GROUPS,)),
            pltpu.SemaphoreType.DMA((LINE,)),
            pltpu.SemaphoreType.DMA((LINE,)),
            pltpu.SemaphoreType.DMA((PIECES,)),
        ],
        compiler_params=pltpu.CompilerParams(
            collective_id=0, has_side_effects=True, vmem_limit_bytes=limit
        ),
        name="gather_kernel",
    )(
        hidden, features, jnp.swapaxes(kv_weight, 1, 2), jnp.swapaxes(mod_table, 1, 2),
        timestep, block_list, block_count,
    )
    return pl.pallas_call(
        attend_kernel,
        out_shape=shape(hidden.shape, bf16),
        in_specs=[hbm, hbm, hbm, smem, smem],
        out_specs=vmem,
        scratch_shapes=[
            pltpu.VMEM((rows, width), bf16),
            pltpu.VMEM((nblk, 3, width), jnp.float32),
            pltpu.VMEM((2 * GROUPS, LIVE, BLK, GW), bf16),
            pltpu.VMEM((rows, width), bf16),
            pltpu.SemaphoreType.DMA((2,)),
            pltpu.SemaphoreType.DMA((LIVE,)),
        ],
        compiler_params=pltpu.CompilerParams(vmem_limit_bytes=limit),
        cost_estimate=pl.CostEstimate(
            flops=4 * LIVE * BLK * BLK * width, bytes_accessed=1 << 22,
            transcendentals=LIVE * BLK * BLK * HEADS,
        ),
        name="attend_kernel",
    )(hin, mods, kv, lists, counts)


def from_behind(block, axis, distance):
    devices = range(lax.axis_size(axis))
    route = [((i - distance) % len(devices), i) for i in devices]
    return lax.ppermute(block, axis, route)


def local(hidden, features, kv_weight, mod_table, timestep, block_list, block_count):
    feature_table = lax.all_gather(features, "frames", axis=0, tiled=True)
    stream = hidden[0].astype(jnp.float32)
    tok_rows = stream.shape[0]
    feature_width = stream.shape[1]
    blocks_here = tok_rows // BLK
    normed = stream * lax.rsqrt(jnp.mean(stream * stream, axis=-1, keepdims=True) + 1e-06)
    levels = mod_table.shape[1]
    onehot = (timestep[0][:, None] == jnp.arange(levels, dtype=jnp.int32)[None, :]).astype(
        jnp.float32
    )
    modulate = jnp.sum(onehot[:, :, None, None] * mod_table[0][None], axis=1)
    normed_blocks = normed.reshape(blocks_here, BLK, feature_width)
    queries = (
        normed_blocks * (1.0 + modulate[:, 1][:, None, :]) + modulate[:, 0][:, None, :]
    ).astype(jnp.bfloat16)
    queries = queries.reshape(blocks_here, BLK, HEADS, HD)
    list_counts = block_count[0]
    list_blocks = block_list[0]
    slot_count = list_blocks.shape[1]
    offsets = jnp.arange(BLK, dtype=jnp.int32)
    inv_root = 1.0 / HD**0.5
    row_index = (list_blocks[:, :, None] * BLK + offsets[None, None, :]).reshape(-1)
    key_mask = jnp.repeat(
        jnp.arange(slot_count, dtype=jnp.int32)[None, :] < list_counts[:, None], BLK, axis=1
    )
    selected = jnp.take(feature_table, row_index, axis=0)
    key_values = jnp.dot(
        selected,
        lax.all_gather(kv_weight[0], "frames", axis=1, tiled=True),
        preferred_element_type=jnp.float32,
    ).astype(jnp.bfloat16)
    key_heads = key_values[:, :feature_width].reshape(-1, HEADS, HD)
    value_heads = key_values[:, feature_width:].reshape(-1, HEADS, HD)
    keys_part = key_heads.reshape(blocks_here, -1, HEADS, HD)
    values_part = value_heads.reshape(blocks_here, -1, HEADS, HD)
    scores = jnp.einsum("bqhd,bkhd->bhqk", queries, keys_part, preferred_element_type=jnp.float32)
    softmax_scores = scores
    softmax_scores = jnp.where(
        key_mask[:, None, None, :], softmax_scores * inv_root, jnp.float32(-1e30)
    )
    top_score = jnp.max(softmax_scores, axis=-1, keepdims=True)
    expo = jnp.exp(softmax_scores - top_score)
    weights = (expo / jnp.sum(expo, axis=-1, keepdims=True)).astype(jnp.bfloat16)
    mixed_heads = jnp.einsum(
        "bhqk,bkhd->bqhd", weights, values_part, preferred_element_type=jnp.float32
    )
    part_blocks = blocks_here - 0
    mixed_rows = mixed_heads.reshape(part_blocks * BLK, feature_width)
    gate_rows = jnp.repeat(modulate[0:blocks_here, 2], BLK, axis=0)
    result = (stream + gate_rows * mixed_rows).astype(jnp.bfloat16)
    handed = from_behind(result[None], "segment", 1)
    return handed


def solution(mesh):
    placed = (
        P("segment", "frames", None),
        P("frames", None),
        P("segment", None, "frames"),
        P("segment", None, None, None),
        P("segment", "frames"),
        P("segment", "frames", None),
        P("segment", "frames"),
    )
    step = local
    if mesh.shape["frames"] == LINE * LANES * CORES and mesh.shape["segment"] == 2:
        step = functools.partial(local_line, mesh.shape["segment"])
    return jax.shard_map(
        step, mesh=mesh, in_specs=placed, out_specs=P("segment", "frames", None), check_vma=False
    )
```

```python
import functools

import jax
import jax.numpy as jnp
from jax import lax
from jax.experimental import pallas as pl
from jax.experimental.pallas import tpu as pltpu
from jax.sharding import PartitionSpec as P

HEADS = 12
HD = 128
BLK = 64
MESH = pl.DeviceIdType.MESH
LINE, LANES, CORES = 4, 2, 2
GROUPS = 4
GH = HEADS // GROUPS
GW = GH * HD
LIVE = 10
NT_DIMS = (((1,), (1,)), ((), ()))


def gather_kernel(
    segs,
    hidden_ref, feat_ref, w_ref, mod_ref, ts_ref, list_ref, count_ref,
    kv_out, hin, min_, list_in, count_in,
    fbuf, wbuf, kv, mst, mbuf,
    zsem, ysem, csem, rsem, xsend, xrecv, lsem, ksem, fsend, frecv,
):
    me = lax.axis_index("frames")
    seg = lax.axis_index("segment")
    c = me % CORES
    y = (me // CORES) % LANES
    z = me // (CORES * LANES)
    nxt = (seg + 1) % segs
    half = wbuf.shape[1]
    nblk = mst.shape[0]

    def shard(zz, yy, cc):
        return (zz * LANES + yy) * CORES + cc

    across = shard(z, 1 - y, c)

    def slot(p, s):
        return fbuf.at[s] if p == 0 else wbuf.at[2 * s + (p - 1)]

    def remote(src, dst, send, recv, **to):
        return pltpu.make_async_remote_copy(
            src_ref=src, dst_ref=dst, send_sem=send, recv_sem=recv,
            device_id=to, device_id_type=MESH,
        )

    def copy(p, s, to, sem):
        return remote(slot(p, s), slot(p, s), sem, rsem.at[p, s], frames=to)

    def z_copy(p, s, t, up):
        return copy(p, s, shard(z + 1 if up else z - 1, y, c), zsem.at[p, t, int(up)])

    def feature_half(s, part):
        rows = fbuf.shape[1] // 2
        return fbuf.at[s, pl.ds(pl.multiple_of(part * rows, rows), rows)]

    def y_copy(p, zz):
        s = shard(zz, y, c)
        if p > 0:
            return copy(p, s, across, ysem.at[p, zz])
        piece = feature_half(s, seg)
        return remote(piece, piece, ysem.at[p, zz], rsem.at[p, s], frames=across)

    def x_copy(zz):
        piece = feature_half(shard(zz, 1 - y, c), seg)
        return remote(piece, piece, fsend.at[zz], frecv.at[zz], segment=nxt)

    def c_copy(p, zz, yy):
        return copy(p, shard(zz, yy, c), shard(z, y, 1 - c), csem.at[p, zz * LANES + yy])

    def wait_recv(p, s):
        copy(p, s, across, csem.at[0, 0]).wait_recv()

    def hand_on():
        first = hin.shape[0] // 2
        return [
            remote(w_ref.at[0, pl.ds(0, half)], wbuf.at[2 * me], xsend.at[0], rsem.at[1, me], segment=nxt),
            remote(w_ref.at[0, pl.ds(half, half)], wbuf.at[2 * me + 1], xsend.at[1], rsem.at[2, me], segment=nxt),
            remote(
                hidden_ref.at[0, pl.ds(0, first)], hin.at[pl.ds(0, first)],
                xsend.at[2], xrecv.at[2], segment=nxt,
            ),
            remote(list_ref, list_in, xsend.at[3], xrecv.at[3], segment=nxt),
            remote(count_ref, count_in, xsend.at[4], xrecv.at[4], segment=nxt),
            remote(mst, min_, xsend.at[5], xrecv.at[5], segment=nxt),
            remote(
                hidden_ref.at[0, pl.ds(first, first)], hin.at[pl.ds(first, first)],
                xsend.at[6], xrecv.at[6], segment=nxt,
            ),
        ]

    def z_event(p, t):
        if t == 0:
            if p > 0:
                wait_recv(p, me)
            y_copy(p, z).start()

            @pl.when(z > 0)
            def _():
                z_copy(p, me, 0, False).start()

            @pl.when(z < LINE - 1)
            def _():
                z_copy(p, me, 0, True).start()

            c_copy(p, z, y).start()
            return

        @pl.when(z - t >= 0)
        def _():
            s = shard(z - t, y, c)
            wait_recv(p, s)
            y_copy(p, z - t).start()

            @pl.when(z < LINE - 1)
            def _():
                z_copy(p, s, t, True).start()

            c_copy(p, z - t, y).start()

        @pl.when(z + t <= LINE - 1)
        def _():
            s = shard(z + t, y, c)
            wait_recv(p, s)
            y_copy(p, z + t).start()

            @pl.when(z > 0)
            def _():
                z_copy(p, s, t, False).start()

            c_copy(p, z + t, y).start()

    def y_event(p, t):
        def arrive(zz):
            s = shard(zz, 1 - y, c)
            if p > 0:
                wait_recv(p, s)
                c_copy(p, zz, 1 - y).start()
                return
            piece = feature_half(s, seg)
            remote(piece, piece, fsend.at[zz], rsem.at[p, s], frames=across).wait_recv()
            x_copy(zz).start()

        at_distance(t, arrive)

    def x_event(t):
        def arrive(zz):
            x_copy(zz).wait_recv()
            c_copy(0, zz, 1 - y).start()

        at_distance(t, arrive)

    def at_distance(t, arrive):
        if t == 0:
            arrive(z)
            return

        @pl.when(z - t >= 0)
        def _():
            arrive(z - t)

        @pl.when(z + t <= LINE - 1)
        def _():
            arrive(z + t)

    def keep(zz, yy):
        pair = zz * LANES + yy
        return pltpu.make_async_copy(kv.at[pair], kv_out.at[pair], ksem.at[pair])

    def project(zz, yy):
        for p in (1, 2):
            wait_recv(p, shard(zz, yy, 1 - c))
        pair = zz * LANES + yy
        weight = wbuf[pl.ds(4 * pair, 4)].reshape(4 * half, wbuf.shape[2])
        step = fbuf.shape[0] // 2

        def one(r, carry):
            f = fbuf[pl.ds(r * step, step)].reshape(step * fbuf.shape[1], fbuf.shape[2])
            part = lax.dot_general(f, weight, NT_DIMS, preferred_element_type=jnp.float32)
            kv[pair, pl.ds(r * step, step)] = part.astype(jnp.bfloat16).reshape(step, BLK, GW)
            return carry

        lax.fori_loop(0, 2, one, 0)
        keep(zz, yy).start()

    load = pltpu.make_async_copy(feat_ref, fbuf.at[me], lsem.at[0])
    load.start()
    table = pltpu.make_async_copy(mod_ref.at[0], mbuf, lsem.at[1])
    table.start()
    barrier = pltpu.get_barrier_semaphore()

    def greet(**where):
        pl.semaphore_signal(barrier, inc=1, device_id=where, device_id_type=MESH)

    @pl.when(z > 0)
    def _():
        greet(frames=shard(z - 1, y, c))

    @pl.when(z < LINE - 1)
    def _():
        greet(frames=shard(z + 1, y, c))

    greet(frames=across)
    greet(frames=shard(z, y, 1 - c))
    greet(segment=nxt)
    if segs > 2:
        greet(segment=(seg + segs - 1) % segs)
    ends = jnp.where(z == 0, 1, 0) + jnp.where(z == LINE - 1, 1, 0)
    pl.semaphore_wait(barrier, (5 if segs > 2 else 4) + 1 - ends)

    handed = hand_on()
    handed[0].start()
    handed[1].start()
    load.wait()
    z_event(0, 0)
    for item in handed[2:5]:
        item.start()
    table.wait()
    for b in range(nblk):
        level = ts_ref[0, b]
        for i in range(3):
            mst[b, i:i + 1, :] = mbuf[i, level].reshape(1, -1)
    handed[5].start()
    z_event(0, 1)
    z_event(1, 0)
    z_event(0, 2)
    z_event(2, 0)
    y_event(0, 0)
    z_event(1, 1)
    y_event(0, 1)
    z_event(0, 3)
    z_event(2, 1)
    y_event(0, 2)
    z_event(1, 2)
    y_event(1, 0)
    y_event(0, 3)
    handed[6].start()
    z_event(2, 2)
    x_event(0)
    x_event(1)
    y_event(2, 0)
    x_event(2)
    x_event(3)
    y_event(1, 1)
    for zz in range(LINE):
        for yy in range(LANES):
            wait_recv(0, shard(zz, yy, 1 - c))
    order = (
        z,
        jnp.where(z == 0, 1, z - 1),
        jnp.where(z == 3, 1, jnp.where(z == 2, 3, 2)),
        jnp.where(z < 2, 3, 0),
    )
    project(order[0], y)
    z_event(1, 3)
    y_event(2, 1)
    project(order[1], y)
    z_event(2, 3)
    project(order[0], 1 - y)
    y_event(1, 2)
    project(order[2], y)
    y_event(2, 2)
    project(order[1], 1 - y)
    y_event(1, 3)
    project(order[3], y)
    y_event(2, 3)
    project(order[2], 1 - y)
    project(order[3], 1 - y)
    for p in range(3):
        for t in range(LINE - 1):
            @pl.when((z - t >= 0) & (z < LINE - 1))
            def _():
                z_copy(p, me, t, True).wait_send()

            @pl.when((z + t <= LINE - 1) & (z > 0))
            def _():
                z_copy(p, me, t, False).wait_send()

        for zz in range(LINE):
            y_copy(p, zz).wait_send()
            for yy in range(LANES):
                c_copy(p, zz, yy).wait_send()
    for zz in range(LINE):
        x_copy(zz).wait_send()
    for item in handed[:2]:
        item.wait_send()
    for item in handed[2:]:
        item.wait()
    for zz in range(LINE):
        for yy in range(LANES):
            keep(zz, yy).wait()


def attend_kernel(
    hidden_ref, mod_ref, kv_ref, list_ref, count_ref, out_ref, hbuf, mbuf, kv, qbuf, lsem, ksem
):
    rows = hbuf.shape[0]
    nblk = rows // BLK
    sel = list_ref.shape[2]

    def entry(b, j, at):
        return pltpu.make_async_copy(kv_ref.at[:, list_ref[0, b, j]], kv.at[:, at], ksem.at[at])

    loads = [
        pltpu.make_async_copy(hidden_ref, hbuf, lsem.at[0]),
        pltpu.make_async_copy(mod_ref, mbuf, lsem.at[1]),
    ]
    for load in loads:
        load.start()
    start = 0
    for b in range(nblk):
        live = count_ref[0, b]
        for j in range(sel):
            @pl.when(j < live)
            def _():
                entry(b, j, start + j).start()
        start = start + live
    for load in loads:
        load.wait()
    for b in range(nblk):
        span = slice(b * BLK, (b + 1) * BLK)
        x = hbuf[span, :].astype(jnp.float32)
        normed = x * lax.rsqrt(jnp.mean(x * x, axis=-1, keepdims=True) + 1e-06)
        mod = mbuf[b]
        qbuf[span, :] = (normed * (1.0 + mod[1:2]) + mod[0:1]).astype(jnp.bfloat16)

    def block(b, start, live):
        span = pl.ds(pl.multiple_of(b * BLK, BLK), BLK)
        q = qbuf[span, :]
        mod = mbuf[b]

        def attend(n):
            for j in range(n):
                entry(b, j, start + j).wait()
            keys = [kv[g, pl.ds(start, n)].reshape(n * BLK, GW) for g in range(GROUPS)]
            values = [kv[GROUPS + g, pl.ds(start, n)].reshape(n * BLK, GW) for g in range(GROUPS)]
            parts = [(h // GH, slice(h % GH * HD, (h % GH + 1) * HD)) for h in range(HEADS)]
            scores = jnp.concatenate([
                lax.dot_general(
                    q[:, h * HD:(h + 1) * HD], keys[g][:, part], NT_DIMS,
                    preferred_element_type=jnp.float32,
                )
                for h, (g, part) in enumerate(parts)
            ], axis=0) * (1.0 / HD ** 0.5)
            expo = jnp.exp(scores - jnp.max(scores, axis=-1, keepdims=True))
            weights = (expo * (1.0 / jnp.sum(expo, axis=-1, keepdims=True))).astype(jnp.bfloat16)
            mixed = jnp.concatenate([
                jnp.dot(
                    weights[h * BLK:(h + 1) * BLK], values[g][:, part],
                    preferred_element_type=jnp.float32,
                )
                for h, (g, part) in enumerate(parts)
            ], axis=1)
            out_ref[0, span, :] = (
                hbuf[span, :].astype(jnp.float32) + mod[2:3] * mixed
            ).astype(jnp.bfloat16)

        for n in range(1, sel + 1):
            @pl.when(live == n)
            def _():
                attend(n)

    def one(b, start):
        live = count_ref[0, b]
        block(b, start, live)
        return start + live

    lax.fori_loop(0, nblk, one, jnp.int32(0))


def local_line(segs, hidden, features, kv_weight, mod_table, timestep, block_list, block_count):
    n = LINE * LANES * CORES
    rows, width = hidden.shape[1:]
    frows, fwidth = features.shape
    half = kv_weight.shape[2] // 2
    nblk = rows // BLK
    hbm = pl.BlockSpec(memory_space=pl.ANY)
    vmem = pl.BlockSpec(memory_space=pltpu.VMEM)
    smem = pl.BlockSpec(memory_space=pltpu.SMEM)
    bf16 = jnp.bfloat16
    shape = jax.ShapeDtypeStruct
    kv_shape = (2 * GROUPS, n * frows // BLK, BLK, GW)
    limit = 60 * 1024 * 1024
    kv, hin, mods, lists, counts = pl.pallas_call(
        functools.partial(gather_kernel, segs),
        out_shape=(
            shape(kv_shape, bf16),
            shape((rows, width), bf16),
            shape((nblk, 3, width), jnp.float32),
            shape(block_list.shape, jnp.int32),
            shape(block_count.shape, jnp.int32),
        ),
        in_specs=[hbm, hbm, hbm, hbm, smem, smem, smem],
        out_specs=(hbm, hbm, hbm, smem, smem),
        scratch_shapes=[
            pltpu.VMEM((n, frows, fwidth), bf16),
            pltpu.VMEM((2 * n, half, fwidth), bf16),
            pltpu.VMEM(kv_shape, bf16),
            pltpu.VMEM((nblk, 3, width), jnp.float32),
            pltpu.VMEM((3, mod_table.shape[1], width), jnp.float32),
            pltpu.SemaphoreType.DMA((3, LINE, 2)),
            pltpu.SemaphoreType.DMA((3, LINE)),
            pltpu.SemaphoreType.DMA((3, LINE * LANES)),
            pltpu.SemaphoreType.DMA((3, n)),
            pltpu.SemaphoreType.DMA((7,)),
            pltpu.SemaphoreType.DMA((7,)),
            pltpu.SemaphoreType.DMA((2,)),
            pltpu.SemaphoreType.DMA((2 * GROUPS,)),
            pltpu.SemaphoreType.DMA((LINE,)),
            pltpu.SemaphoreType.DMA((LINE,)),
        ],
        compiler_params=pltpu.CompilerParams(
            collective_id=0, has_side_effects=True, vmem_limit_bytes=limit
        ),
        name="gather_kernel",
    )(
        hidden, features, jnp.swapaxes(kv_weight, 1, 2), jnp.swapaxes(mod_table, 1, 2),
        timestep, block_list, block_count,
    )
    return pl.pallas_call(
        attend_kernel,
        out_shape=shape(hidden.shape, bf16),
        in_specs=[hbm, hbm, hbm, smem, smem],
        out_specs=vmem,
        scratch_shapes=[
            pltpu.VMEM((rows, width), bf16),
            pltpu.VMEM((nblk, 3, width), jnp.float32),
            pltpu.VMEM((2 * GROUPS, LIVE, BLK, GW), bf16),
            pltpu.VMEM((rows, width), bf16),
            pltpu.SemaphoreType.DMA((2,)),
            pltpu.SemaphoreType.DMA((LIVE,)),
        ],
        compiler_params=pltpu.CompilerParams(vmem_limit_bytes=limit),
        cost_estimate=pl.CostEstimate(
            flops=4 * LIVE * BLK * BLK * width, bytes_accessed=1 << 22,
            transcendentals=LIVE * BLK * BLK * HEADS,
        ),
        name="attend_kernel",
    )(hin, mods, kv, lists, counts)


def from_behind(block, axis, distance):
    devices = range(lax.axis_size(axis))
    route = [((i - distance) % len(devices), i) for i in devices]
    return lax.ppermute(block, axis, route)


def local(hidden, features, kv_weight, mod_table, timestep, block_list, block_count):
    feature_table = lax.all_gather(features, "frames", axis=0, tiled=True)
    stream = hidden[0].astype(jnp.float32)
    tok_rows = stream.shape[0]
    feature_width = stream.shape[1]
    blocks_here = tok_rows // BLK
    normed = stream * lax.rsqrt(jnp.mean(stream * stream, axis=-1, keepdims=True) + 1e-06)
    levels = mod_table.shape[1]
    onehot = (timestep[0][:, None] == jnp.arange(levels, dtype=jnp.int32)[None, :]).astype(
        jnp.float32
    )
    modulate = jnp.sum(onehot[:, :, None, None] * mod_table[0][None], axis=1)
    normed_blocks = normed.reshape(blocks_here, BLK, feature_width)
    queries = (
        normed_blocks * (1.0 + modulate[:, 1][:, None, :]) + modulate[:, 0][:, None, :]
    ).astype(jnp.bfloat16)
    queries = queries.reshape(blocks_here, BLK, HEADS, HD)
    list_counts = block_count[0]
    list_blocks = block_list[0]
    slot_count = list_blocks.shape[1]
    offsets = jnp.arange(BLK, dtype=jnp.int32)
    inv_root = 1.0 / HD**0.5
    row_index = (list_blocks[:, :, None] * BLK + offsets[None, None, :]).reshape(-1)
    key_mask = jnp.repeat(
        jnp.arange(slot_count, dtype=jnp.int32)[None, :] < list_counts[:, None], BLK, axis=1
    )
    selected = jnp.take(feature_table, row_index, axis=0)
    key_values = jnp.dot(
        selected,
        lax.all_gather(kv_weight[0], "frames", axis=1, tiled=True),
        preferred_element_type=jnp.float32,
    ).astype(jnp.bfloat16)
    key_heads = key_values[:, :feature_width].reshape(-1, HEADS, HD)
    value_heads = key_values[:, feature_width:].reshape(-1, HEADS, HD)
    keys_part = key_heads.reshape(blocks_here, -1, HEADS, HD)
    values_part = value_heads.reshape(blocks_here, -1, HEADS, HD)
    scores = jnp.einsum("bqhd,bkhd->bhqk", queries, keys_part, preferred_element_type=jnp.float32)
    softmax_scores = scores
    softmax_scores = jnp.where(
        key_mask[:, None, None, :], softmax_scores * inv_root, jnp.float32(-1e30)
    )
    top_score = jnp.max(softmax_scores, axis=-1, keepdims=True)
    expo = jnp.exp(softmax_scores - top_score)
    weights = (expo / jnp.sum(expo, axis=-1, keepdims=True)).astype(jnp.bfloat16)
    mixed_heads = jnp.einsum(
        "bhqk,bkhd->bqhd", weights, values_part, preferred_element_type=jnp.float32
    )
    part_blocks = blocks_here - 0
    mixed_rows = mixed_heads.reshape(part_blocks * BLK, feature_width)
    gate_rows = jnp.repeat(modulate[0:blocks_here, 2], BLK, axis=0)
    result = (stream + gate_rows * mixed_rows).astype(jnp.bfloat16)
    handed = from_behind(result[None], "segment", 1)
    return handed


def solution(mesh):
    placed = (
        P("segment", "frames", None),
        P("frames", None),
        P("segment", None, "frames"),
        P("segment", None, None, None),
        P("segment", "frames"),
        P("segment", "frames", None),
        P("segment", "frames"),
    )
    step = local
    if mesh.shape["frames"] == LINE * LANES * CORES and mesh.shape["segment"] == 2:
        step = functools.partial(local_line, mesh.shape["segment"])
    return jax.shard_map(
        step, mesh=mesh, in_specs=placed, out_specs=P("segment", "frames", None), check_vma=False
    )
```
